32 devices in a mesh: rowa: 4 (over y, x), rowb: 8 (over z, core).
Axes of the slice: x: 2, y: 2, z: 4, core: 2. Of those that a mesh axis runs over, the one named last changes fastest.
Arguments:
- right_side: float32 [12288, 8], P(('rowa', 'rowb')), may hold values from -6 to 6
- leaves: float32 [12288, 384], P(('rowa', 'rowb')), as said below
- bases: float32 [5, 12288, 128], P(None, ('rowa', 'rowb')), may hold values from -0.3125 to 0.3125
- ranks: int32 [31], replicated, may hold values from 64 to 128
Outputs:
- solution: float32 [12288, 8], P(('rowa', 'rowb'))
The draws below stay inside these ranges and needn't reach their ends.
Inputs may be any that keep to these rules, and one draw needn't show every extreme that they name: `ranks`: entry 2^(5 - m) + k - 1 is the rank of node k of level m (levels counted from the leaves, the root at level 5). `leaves`: each leaf block is symmetric positive definite.
All inputs are finite; a program needn't handle non-finite values.
Results may differ from the reference program's by a relative error of at most 0.0001.
Values sent between devices are 32-bit elements; how exact they have to be, the bound alone decides.
No kernel may reach another device: no remote copies, remote signals or barrier semaphores. Data moves between devices by JAX's collectives and lax.ppermute only.
A program may use at most 64 MiB of HBM per device.

```python
import jax
import jax.numpy as jnp
from jax import lax

LEAF = 384
RMAX = 128
NRHS = 8
LEVELS = 5
NTOT = 12288
DEVICES = 32


def draw_leaves(key, part):
    key_locations = jax.random.fold_in(key, 11)
    key_shift = jax.random.fold_in(key, 12)
    block_count = NTOT // LEAF
    side = 0.5 * jnp.sqrt(jnp.float32(LEAF))
    points = jax.random.uniform(key_locations, (block_count, LEAF, 2), jnp.float32) * side
    shift = jnp.exp(jax.random.uniform(key_shift, (block_count, LEAF), jnp.float32, jnp.log(0.5), jnp.log(2.0)))
    squares = jnp.sum(points * points, axis=2)
    inner = jnp.einsum('pid,pjd->pij', points, points)
    squared_distance = squares[:, :, None] + squares[:, None, :] - 2.0 * inner
    kernel = jnp.exp(-0.5 * jnp.maximum(squared_distance, 0.0))
    kernel = 0.5 * (kernel + jnp.swapaxes(kernel, 1, 2))
    eye_block = jnp.eye(LEAF, dtype=jnp.float32)[None]
    matrix = kernel + eye_block * shift[:, :, None]
    return matrix.reshape(NTOT, LEAF)


def touch_ends(entries, rng, least, top_value):
    longest = entries.shape.index(max(entries.shape))
    spots = []
    for shift in (0, 1):
        where = [jax.random.randint(jax.random.fold_in(rng, axis), (), 0, length) for axis, length in enumerate(entries.shape)]
        where[longest] = (where[longest] + shift) % entries.shape[longest]
        spots.append(tuple(where))
    return entries.at[spots[0]].set(least).at[spots[1]].set(top_value)


def block_scale(key, shape, shards, low, top_value):
    def one(dim, blocks):
        draws = jax.random.uniform(jax.random.fold_in(jax.random.fold_in(key, 6), dim), (blocks,), jnp.float32, low / len(shards), top_value / len(shards))
        return jnp.repeat(jnp.exp(draws), shape[dim] // blocks).reshape((-1,) + (1,) * (len(shape) - dim - 1))

    factor_of = one(*shards[0])
    for cut in shards[1:]:
        factor_of = factor_of * one(*cut)
    return factor_of


def noise(rng, dims, scale, most, pieces=(), held_as=jnp.bfloat16):
    values = scale * jax.random.normal(rng, dims, jnp.float32)
    if pieces:
        values = values * block_scale(rng, dims, pieces, -0.22, 0.18)
    return jnp.clip(values, -most, most).astype(held_as)


def setup_inputs(seed: int = 0) -> dict:
    splits = jax.random.split(jax.random.key(seed), 5)
    right_side = noise(splits[0], (NTOT, NRHS), 1.0, 6.0, ((0, 32),), jnp.float32)
    leaves = draw_leaves(jax.random.fold_in(splits[4], 71), 0)
    bases = noise(splits[2], (LEVELS, NTOT, RMAX), LEAF ** -0.5, 0.3125, ((1, 32),), jnp.float32)
    ranks = touch_ends(jax.random.randint(splits[3], (DEVICES - 1,), RMAX // 2, RMAX + 1), jax.random.fold_in(splits[3], 1), RMAX // 2, RMAX).astype(jnp.int32)
    return {"right_side": right_side, "leaves": leaves, "bases": bases, "ranks": ranks}


PRECISION_HIGH = lax.Precision.HIGHEST

def factored_system_solve(factor, values):
    half = lax.linalg.triangular_solve(factor, values, left_side=True, lower=True)
    return lax.linalg.triangular_solve(factor, half, left_side=True, lower=True, transpose_a=True)

def leaf_solve(inputs):
    block, rhs_block, basis_block = inputs
    factor = jnp.linalg.cholesky(block)
    return (factored_system_solve(factor, rhs_block), factored_system_solve(factor, basis_block))

def reference(right_side, leaves, bases, ranks):
    block_count = NTOT // LEAF
    columns = jnp.arange(RMAX)
    masked_values = []
    for tree_level in range(1, LEVELS + 1):
        node_index = jnp.arange(block_count) // 2 ** tree_level
        node_rank = ranks[2 ** (LEVELS - tree_level) + node_index - 1]
        keep = (columns[None, :] < node_rank[:, None]).astype(jnp.float32)
        masked_values.append(bases[tree_level - 1].reshape(block_count, LEAF, RMAX) * keep[:, None, :])
    stacked = jnp.concatenate(masked_values, axis=2)
    blocks = leaves.reshape(block_count, LEAF, LEAF)
    solution, corrected = lax.map(leaf_solve, (blocks, right_side.reshape(block_count, LEAF, NRHS), stacked))
    for tree_level in range(1, LEVELS + 1):
        node_count = block_count // 2 ** tree_level
        covered_rows = LEAF * 2 ** tree_level
        level_basis = masked_values[tree_level - 1].reshape(node_count, covered_rows, RMAX)
        current_all = corrected.reshape(node_count, covered_rows, -1)
        current_rhs = solution.reshape(node_count, covered_rows, NRHS)
        products = jnp.einsum('qir,qic->qrc', level_basis, current_all, precision=PRECISION_HIGH)
        right_terms = jnp.einsum('qir,qic->qrc', level_basis, current_rhs, precision=PRECISION_HIGH)
        capacitance = jnp.eye(RMAX, dtype=products.dtype)[None] + products[:, :, :RMAX]
        cap_factor = jnp.linalg.cholesky(capacitance)
        current = current_all[:, :, :RMAX]
        coef_rhs = jax.vmap(factored_system_solve)(cap_factor, right_terms)
        current_rhs = current_rhs - jnp.einsum('qir,qrc->qic', current, coef_rhs, precision=PRECISION_HIGH)
        solution = current_rhs.reshape(block_count, LEAF, NRHS)
        if tree_level < LEVELS:
            coef_rest = jax.vmap(factored_system_solve)(cap_factor, products[:, :, RMAX:])
            remaining = current_all[:, :, RMAX:] - jnp.einsum('qir,qrc->qic', current, coef_rest, precision=PRECISION_HIGH)
            corrected = remaining.reshape(block_count, LEAF, -1)
    return solution.reshape(NTOT, NRHS)
```

```python
import functools

import jax
import jax.numpy as jnp
from jax import lax
from jax.experimental import pallas as pl
from jax.experimental.pallas import tpu as pltpu
from jax.sharding import PartitionSpec as P

HIGHEST = lax.Precision.HIGHEST
F32 = jnp.float32
BF16 = jnp.bfloat16
STEP = 16
VMEM_LIMIT = 48 * 1024 * 1024


def dot(left, right):
    return jnp.dot(left, right, precision=HIGHEST, preferred_element_type=F32)


def dot_nt(left, right):
    return lax.dot_general(
        left, right, (((1,), (1,)), ((), ())), precision=HIGHEST, preferred_element_type=F32
    )


def split3(value):
    high = value.astype(BF16).astype(F32)
    rest = value - high
    middle = rest.astype(BF16).astype(F32)
    return high, middle, rest - middle


def reciprocal(value):
    guess = pltpu.reciprocal(value, approx=True)
    return guess * (2.0 - value * guess)


def inverse(matrix):
    size = matrix.shape[0]
    lane = lax.broadcasted_iota(jnp.int32, (STEP, size), 1)
    sub = lax.broadcasted_iota(jnp.int32, (STEP, size), 0)
    lane_all = lax.broadcasted_iota(jnp.int32, (size, size), 1)
    sub_all = lax.broadcasted_iota(jnp.int32, (size, size), 0)
    for start in range(0, size, STEP):
        stop = start + STEP
        rows = matrix[start:stop, :]
        pivots = [
            jnp.broadcast_to(rows[:, start + index : start + index + 1], (STEP, size))
            for index in range(STEP)
        ]
        inside = (lane >= start) & (lane < stop)
        panel = jnp.where(inside, jnp.where(lane - start == sub, 1.0, 0.0), rows)
        for index in range(STEP):
            scale = reciprocal(pivots[index][index : index + 1, :])
            factor = jnp.where(sub == index, -1.0, pivots[index])
            panel = jnp.where(sub == index, 0.0, panel) - factor * (panel[index : index + 1] * scale)
            for later in range(index + 1, STEP):
                row = pivots[later][index : index + 1] * scale
                pivots[later] = jnp.where(sub == index, 0.0, pivots[later]) - factor * row
        row_inside = (sub_all >= start) & (sub_all < stop)
        lane_inside = (lane_all >= start) & (lane_all < stop)
        column = jnp.where(row_inside, 0.0, matrix)[:, start:stop]
        base = jnp.where(row_inside | lane_inside, 0.0, matrix)
        c_high, c_mid, c_low = split3(column)
        p_high, p_mid, p_low = split3(panel)
        left = jnp.concatenate([c_high, c_high, c_mid, c_high, c_mid, c_low], axis=1).astype(BF16)
        right = jnp.concatenate([p_high, p_mid, p_high, p_low, p_mid, p_high], axis=0).astype(BF16)
        matrix = base - jnp.dot(left, right, preferred_element_type=F32)
        pieces = [matrix[:start]] if start else []
        pieces.append(panel)
        if stop < size:
            pieces.append(matrix[stop:])
        matrix = jnp.concatenate(pieces, axis=0)
    return matrix


def leaf_kernel(levels, width, blocks, ranks_ref, place_ref, rhs_ref, leaf_ref, bases_ref, *refs):
    head_ref, tail_ref, scaled_ref, lower_ref, v_ref = refs
    nrhs = rhs_ref.shape[1]
    place = place_ref[0]
    sub = lax.broadcasted_iota(jnp.int32, (width, width), 0)
    rows = levels * width
    for block in range(blocks):
        span = slice(block * width, (block + 1) * width)
        for level in range(1, levels + 1):
            rank = ranks_ref[2 ** (levels - level) + lax.shift_right_logical(place, level) - 1]
            piece = bases_ref[level - 1, span, :].T
            v_ref[block, (level - 1) * width : level * width, :] = jnp.where(sub < rank, piece, 0.0)
        v_ref[block, rows : rows + nrhs, :] = rhs_ref[span, :].T
    schur = {}
    for first in range(blocks):
        for second in range(first, blocks):
            schur[first, second] = leaf_ref[
                first * width : (first + 1) * width, second * width : (second + 1) * width
            ]
    for block in range(blocks):
        inv = inverse(schur[block, block])
        values = v_ref[block]
        scaled = dot(values, inv)
        scaled_ref[block] = scaled
        upper = {}
        for later in range(block + 1, blocks):
            upper[later] = dot(inv, schur[block, later])
            lower_ref[block, later - 1] = upper[later]
            v_ref[later] = v_ref[later] - dot(scaled, schur[block, later])
        for first in range(block + 1, blocks):
            for second in range(first, blocks):
                product = lax.dot_general(
                    schur[block, first],
                    upper[second],
                    (((0,), (0,)), ((), ())),
                    precision=HIGHEST,
                    preferred_element_type=F32,
                )
                schur[first, second] = schur[first, second] - product
        offset = 0
        for level in range(1, levels + 1):
            low = (level - 1) * width
            product = dot_nt(values[low:], scaled[low : low + width])
            if level == 1:
                target, span = head_ref, slice(0, product.shape[0])
            else:
                target, span = tail_ref, slice(offset, offset + product.shape[0])
                offset += product.shape[0]
            if block == 0:
                target[span, :] = product
            else:
                target[span, :] = target[span, :] + product


def pivot_kernel(width, own_ref, other_ref, rest_ref, coef_ref):
    total = own_ref[...] + other_ref[...]
    row = lax.broadcasted_iota(jnp.int32, (width, width), 0)
    column = lax.broadcasted_iota(jnp.int32, (width, width), 1)
    inv = inverse(total[:width] + jnp.where(row == column, 1.0, 0.0))
    rest = total[width:]
    rest_ref[...] = rest
    coef_ref[...] = dot(rest, inv)


def update_kernel(width, left, own_ref, other_ref, rest_ref, coef_ref, head_ref, *refs):
    offset = 0
    for level in range(left):
        low = level * width
        count = coef_ref.shape[0] - low
        span = slice(offset, offset + count)
        product = dot_nt(coef_ref[low:, :], rest_ref[low : low + width, :])
        value = own_ref[span, :] + other_ref[span, :] - product
        if level == 0:
            head_ref[...] = value
        else:
            refs[0][offset - head_ref.shape[0] : offset - head_ref.shape[0] + count, :] = value
        offset += count


def back_kernel(levels, width, blocks, scaled_ref, lower_ref, out_ref):
    values = [None] * blocks
    for block in reversed(range(blocks)):
        value = scaled_ref[block]
        for later in range(block + 1, blocks):
            value = value - dot_nt(values[later], lower_ref[block, later - 1])
        values[block] = value
        out_ref[:, block * width : (block + 1) * width] = value


def final_kernel(levels, width, weights_ref, *refs):
    coef_refs, out_ref = refs[:-1], refs[-1]
    known = []
    for level in reversed(range(levels)):
        coef = coef_refs[level]
        count = (levels - 1 - level) * width
        value = coef[count:, :]
        for index, later in enumerate(known):
            low = (len(known) - 1 - index) * width
            value = value - dot(later, coef[low : low + width, :])
        known.append(value)
    rows = levels * width
    result = weights_ref[rows:, :]
    for level in range(levels):
        result = result - dot(
            known[levels - 1 - level], weights_ref[level * width : (level + 1) * width, :]
        )
    out_ref[...] = result.T


def call(kernel, shapes, *operands, flops=0, smem=0, scratch=()):
    space = [pl.BlockSpec(memory_space=pltpu.SMEM)] * smem
    space += [pl.BlockSpec(memory_space=pltpu.VMEM)] * (len(operands) - smem)
    outs = [jax.ShapeDtypeStruct(shape, F32) for shape in shapes]
    return pl.pallas_call(
        kernel,
        out_shape=outs,
        in_specs=space,
        out_specs=[pl.BlockSpec(memory_space=pltpu.VMEM)] * len(outs),
        scratch_shapes=list(scratch),
        compiler_params=pltpu.CompilerParams(vmem_limit_bytes=VMEM_LIMIT),
        cost_estimate=pl.CostEstimate(flops=flops, bytes_accessed=0, transcendentals=0),
    )(*operands)


def partner(value, tree_level, inner_bits):
    bit = tree_level - 1
    axis, stride = ("rowb", bit) if bit < inner_bits else ("rowa", bit - inner_bits)
    mask = 2**stride
    pairs = [(source, source ^ mask) for source in range(lax.axis_size(axis))]
    return lax.ppermute(value, axis, pairs)


def body(right_side, leaves, bases, ranks):
    levels = bases.shape[0]
    leaf_rows = leaves.shape[0]
    width = bases.shape[2]
    nrhs = right_side.shape[1]
    blocks = leaf_rows // width
    inner_bits = lax.axis_size("rowb").bit_length() - 1
    place = lax.axis_index("rowa") * lax.axis_size("rowb") + lax.axis_index("rowb")
    place = place.astype(jnp.int32).reshape(1)
    rows = levels * width + nrhs
    counts = [rows - level * width for level in range(levels)]
    head, tail, scaled, lower = call(
        functools.partial(leaf_kernel, levels, width, blocks),
        [
            (counts[0], width),
            (sum(counts[1:]), width),
            (blocks, rows, width),
            (blocks, max(blocks - 1, 1), width, width),
        ],
        ranks,
        place,
        right_side,
        leaves,
        bases,
        smem=2,
        scratch=[pltpu.VMEM((blocks, rows, width), F32)],
    )
    coefs = []
    for level in range(levels):
        other_head = partner(head, level + 1, inner_bits)
        if level < levels - 1:
            other_tail = partner(tail, level + 1, inner_bits)
        if level == 0:
            (weights,) = call(
                functools.partial(back_kernel, levels, width, blocks),
                [(rows, leaf_rows)],
                scaled,
                lower,
            )
        count = counts[level] - width
        rest, coef = call(
            functools.partial(pivot_kernel, width),
            [(count, width), (count, width)],
            head,
            other_head,
        )
        coefs.append(coef)
        if level < levels - 1:
            shapes = [(counts[level + 1], width)]
            if level < levels - 2:
                shapes.append((sum(counts[level + 2 :]), width))
            result = call(
                functools.partial(update_kernel, width, levels - 1 - level),
                shapes,
                tail,
                other_tail,
                rest,
                coef,
            )
            head = result[0]
            tail = result[1] if level < levels - 2 else None
    (solution_rows,) = call(
        functools.partial(final_kernel, levels, width), [(leaf_rows, nrhs)], weights, *coefs
    )
    return solution_rows


def solution(mesh):
    placed = (
        P(("rowa", "rowb"), None),
        P(("rowa", "rowb"), None),
        P(None, ("rowa", "rowb"), None),
        P(),
    )
    return jax.shard_map(
        body, mesh=mesh, in_specs=placed, out_specs=P(("rowa", "rowb"), None), check_vma=False
    )
```

```python
import functools

import jax
import jax.numpy as jnp
from jax import lax
from jax.experimental import pallas as pl
from jax.experimental.pallas import tpu as pltpu
from jax.sharding import PartitionSpec as P

HIGHEST = lax.Precision.HIGHEST
F32 = jnp.float32
BF16 = jnp.bfloat16
STEP = 16
VMEM_LIMIT = 48 * 1024 * 1024


def dot(left, right):
    return jnp.dot(left, right, precision=HIGHEST, preferred_element_type=F32)


def dot_nt(left, right):
    return lax.dot_general(
        left, right, (((1,), (1,)), ((), ())), precision=HIGHEST, preferred_element_type=F32
    )


def split3(value):
    high = value.astype(BF16).astype(F32)
    rest = value - high
    middle = rest.astype(BF16).astype(F32)
    return high, middle, rest - middle


def reciprocal(value):
    guess = pltpu.reciprocal(value, approx=True)
    return guess * (2.0 - value * guess)


def sweep(matrix, first, last):
    size = matrix.shape[0]
    lane = lax.broadcasted_iota(jnp.int32, (STEP, size), 1)
    sub = lax.broadcasted_iota(jnp.int32, (STEP, size), 0)
    lane_all = lax.broadcasted_iota(jnp.int32, (size, size), 1)
    sub_all = lax.broadcasted_iota(jnp.int32, (size, size), 0)
    for start in range(first, last, STEP):
        stop = start + STEP
        rows = matrix[start:stop, :]
        pivots = [
            jnp.broadcast_to(rows[:, start + index : start + index + 1], (STEP, size))
            for index in range(STEP)
        ]
        inside = (lane >= start) & (lane < stop)
        panel = jnp.where(inside, jnp.where(lane - start == sub, 1.0, 0.0), rows)
        for index in range(STEP):
            scale = reciprocal(pivots[index][index : index + 1, :])
            factor = jnp.where(sub == index, -1.0, pivots[index])
            panel = jnp.where(sub == index, 0.0, panel) - factor * (panel[index : index + 1] * scale)
            for later in range(index + 1, STEP):
                row = pivots[later][index : index + 1] * scale
                pivots[later] = jnp.where(sub == index, 0.0, pivots[later]) - factor * row
        row_inside = (sub_all >= start) & (sub_all < stop)
        lane_inside = (lane_all >= start) & (lane_all < stop)
        column = jnp.where(row_inside, 0.0, matrix)[:, start:stop]
        base = jnp.where(row_inside | lane_inside, 0.0, matrix)
        c_high, c_mid, c_low = split3(column)
        p_high, p_mid, p_low = split3(panel)
        left = jnp.concatenate([c_high, c_high, c_mid, c_high, c_mid, c_low], axis=1).astype(BF16)
        right = jnp.concatenate([p_high, p_mid, p_high, p_low, p_mid, p_high], axis=0).astype(BF16)
        matrix = base - jnp.dot(left, right, preferred_element_type=F32)
        pieces = [matrix[:start]] if start else []
        pieces.append(panel)
        if stop < size:
            pieces.append(matrix[stop:])
        matrix = jnp.concatenate(pieces, axis=0)
    return matrix


def inverse(matrix):
    return sweep(matrix, 0, matrix.shape[0])


def add_eye(matrix):
    row = lax.broadcasted_iota(jnp.int32, matrix.shape, 0)
    column = lax.broadcasted_iota(jnp.int32, matrix.shape, 1)
    return matrix + jnp.where(row == column, 1.0, 0.0)


def leaf_kernel(levels, width, blocks, ranks_ref, place_ref, rhs_ref, leaf_hbm, bases_hbm, *refs):
    key_ref, rest_ref, scaled_ref, lower_ref, v_ref, leaf_ref, bases_ref, sem = refs
    nrhs = rhs_ref.shape[0]
    place = place_ref[0]
    sub = lax.broadcasted_iota(jnp.int32, (width, width), 0)
    rows = levels * width
    spans = [slice(block * width, (block + 1) * width) for block in range(blocks)]
    leaf_copies = [
        pltpu.make_async_copy(leaf_hbm.at[span], leaf_ref.at[span], sem.at[index])
        for index, span in enumerate(spans)
    ]
    bases_copy = pltpu.make_async_copy(bases_hbm, bases_ref, sem.at[blocks])
    for copy in leaf_copies:
        copy.start()
    bases_copy.start()
    leaf_copies[0].wait()
    part = sweep(leaf_ref[spans[0], spans[0]], 0, 2 * STEP)
    for copy in leaf_copies[1:]:
        copy.wait()
    bases_copy.wait()
    for block, span in enumerate(spans):
        for level in range(1, levels + 1):
            rank = ranks_ref[2 ** (levels - level) + lax.shift_right_logical(place, level) - 1]
            piece = bases_ref[level - 1, span, :].T
            v_ref[block, (level - 1) * width : level * width, :] = jnp.where(sub < rank, piece, 0.0)
        v_ref[block, rows : rows + nrhs, :] = rhs_ref[:, span]
    schur = {}
    for first in range(blocks):
        for second in range(first, blocks):
            schur[first, second] = leaf_ref[spans[first], spans[second]]
    for block in range(blocks):
        if block == 0:
            inv = sweep(part, 2 * STEP, width)
        else:
            inv = inverse(schur[block, block])
        values = v_ref[block]
        upper = {}
        for later in range(block + 1, blocks):
            upper[later] = dot(inv, schur[block, later])
            lower_ref[block, later - 1] = upper[later]
        for first in range(block + 1, blocks):
            for second in range(first, blocks):
                product = lax.dot_general(
                    schur[block, first],
                    upper[second],
                    (((0,), (0,)), ((), ())),
                    precision=HIGHEST,
                    preferred_element_type=F32,
                )
                schur[first, second] = schur[first, second] - product
        scaled = dot(values, inv)
        scaled_ref[block] = scaled
        for later in range(block + 1, blocks):
            v_ref[later] = v_ref[later] - dot(scaled, schur[block, later])
        offset = 0
        for level in range(1, levels + 1):
            low = (level - 1) * width
            product = dot_nt(values[low:], scaled[low : low + width])
            pieces = [(rest_ref, product)]
            if level == 1:
                pieces = [(key_ref, product[:width]), (rest_ref, product[width:])]
            for target, piece in pieces:
                span = slice(0, width)
                if target is rest_ref:
                    span = slice(offset, offset + piece.shape[0])
                    offset += piece.shape[0]
                if block == 0:
                    target[span, :] = piece
                else:
                    target[span, :] = target[span, :] + piece


def pivot_kernel(first, last, *refs):
    if first == 0:
        matrix = add_eye(refs[0][...] + refs[1][...])
    else:
        matrix = refs[0][...]
    refs[-1][...] = sweep(matrix, first, last)


def near_update(width, count, take, *refs):
    rest_ref, coef_ref, key_ref = refs[-3:]
    inv_ref = refs[-4]
    take(refs[:-4], rest_ref)
    rest = rest_ref[:count]
    coef_ref[...] = dot(rest, inv_ref[...])
    key_ref[...] = rest_ref[count : count + width] - dot_nt(coef_ref[:width], rest_ref[:width])


def take_full(refs, rest_ref):
    own_ref, other_ref = refs
    rows = rest_ref.shape[0]
    rest_ref[...] = own_ref[:rows] + other_ref[:rows]


def take_halves(plan, refs, rest_ref):
    place_ref, own_ref, near_ref, cross_ref = refs
    side = place_ref[0] & 1
    for index, source in ((side, near_ref), (side ^ 1, cross_ref)):
        span = pl.ds(plan.half_at(index), plan.half)
        rest_ref[span, :] = own_ref[span, :] + source[...]


def take_quarters(plan, refs, rest_ref):
    for index, source in enumerate(refs[1:]):
        span = pl.ds(plan.quarter_at((refs[0][0] & 3) ^ index), plan.quarter)
        rest_ref[span, :] = source[...]


def rank_update(width, count, below, rest_ref, coef_ref, put):
    offset = 0
    for level in range(below):
        low = level * width
        start = low + width if level == 0 else low
        if start < count:
            put(offset, dot_nt(coef_ref[start:, :], rest_ref[low : low + width, :]))
        offset += count - start


def far_update(plan, width, count, below, scatter, *refs):
    place_ref, rest_ref, coef_ref, *more = refs
    outs = more[-3:] if scatter else more[-1:]
    pair = more[: -len(outs)]
    skip = count + width

    def put(offset, product):
        span = slice(skip + offset, skip + offset + product.shape[0])
        if pair:
            value = pair[0][span, :] + pair[1][span, :]
        else:
            value = rest_ref[span, :]
        outs[0][offset : offset + product.shape[0], :] = value - product

    rank_update(width, count, below, rest_ref, coef_ref, put)
    if scatter:
        place = place_ref[0]
        outs[1][...] = outs[0][pl.ds(plan.half_at(place & 1), plan.half), :]
        outs[2][...] = outs[0][
            pl.ds(plan.near + plan.quarter_at((place & 3) ^ 2), plan.quarter), :
        ]


def quarter_update(plan, width, count, below, *refs):
    place_ref, rest_ref, coef_ref, own_ref, other_ref, out_ref, product_ref = refs

    def put(offset, product):
        product_ref[offset : offset + product.shape[0], :] = product

    rank_update(width, count, below, rest_ref, coef_ref, put)
    at = plan.quarter_at(place_ref[0] & 3)
    out_ref[...] = (
        own_ref[pl.ds(plan.near + at, plan.quarter), :]
        + other_ref[...]
        - product_ref[pl.ds(at, plan.quarter), :]
    )


def add_kernel(own_ref, other_ref, out_ref):
    out_ref[...] = own_ref[...] + other_ref[...]


def back_kernel(width, blocks, scaled_ref, lower_ref, out_ref):
    values = [None] * blocks
    for block in reversed(range(blocks)):
        value = scaled_ref[block]
        for later in range(block + 1, blocks):
            value = value - dot_nt(values[later], lower_ref[block, later - 1])
        values[block] = value
        out_ref[:, block * width : (block + 1) * width] = value


def final_kernel(levels, width, own_ref, other_ref, weights_ref, *refs):
    coef_refs, out_ref = refs[:-1], refs[-1]
    inv = inverse(add_eye(own_ref[:width] + other_ref[:width]))
    known = [dot(own_ref[width:] + other_ref[width:], inv)]
    for level in reversed(range(levels - 1)):
        coef = coef_refs[level]
        count = (levels - 1 - level) * width
        value = coef[count:, :]
        for index, later in enumerate(known):
            low = (len(known) - 1 - index) * width
            value = value - dot(later, coef[low : low + width, :])
        known.append(value)
    rows = levels * width
    result = weights_ref[rows:, :]
    for level in range(levels):
        result = result - dot(
            known[levels - 1 - level], weights_ref[level * width : (level + 1) * width, :]
        )
    out_ref[...] = result


def call(kernel, shapes, *operands, flops=0, smem=0, hbm=0, scratch=()):
    flops = flops or 2 * 10**9
    space = [pl.BlockSpec(memory_space=pltpu.SMEM)] * smem
    space += [pl.BlockSpec(memory_space=pltpu.VMEM)] * (len(operands) - smem - hbm)
    space += [pl.BlockSpec(memory_space=pltpu.HBM)] * hbm
    outs = [jax.ShapeDtypeStruct(shape, F32) for shape in shapes]
    return pl.pallas_call(
        kernel,
        out_shape=outs,
        in_specs=space,
        out_specs=[pl.BlockSpec(memory_space=pltpu.VMEM)] * len(outs),
        scratch_shapes=list(scratch),
        compiler_params=pltpu.CompilerParams(vmem_limit_bytes=VMEM_LIMIT),
        cost_estimate=pl.CostEstimate(flops=flops, bytes_accessed=flops // 300, transcendentals=0),
    )(*operands)


def flip(value, mask, axis="rowb"):
    pairs = [(source, source ^ mask) for source in range(lax.axis_size(axis))]
    return lax.ppermute(value, axis, pairs)


def partner(value, level, inner_bits):
    if level < inner_bits:
        return flip(value, 2**level)
    return flip(value, 2 ** (level - inner_bits), "rowa")


def up(value, step):
    return -(-value // step) * step


class Plan:
    def __init__(self, near, far):
        self.near, self.far = near, far
        self.half = up(near, 16) // 2
        self.quarter = up(far, 32) // 4

    def half_at(self, side):
        return pl.multiple_of(side * (self.near - self.half), 8)

    def quarter_at(self, index):
        return pl.multiple_of(jnp.minimum(index * self.quarter, self.far - self.quarter), 8)


def body(right_side, leaves, bases, ranks):
    levels = bases.shape[0]
    leaf_rows = leaves.shape[0]
    width = bases.shape[2]
    nrhs = right_side.shape[1]
    blocks = leaf_rows // width
    inner_bits = lax.axis_size("rowb").bit_length() - 1
    place = lax.axis_index("rowa") * lax.axis_size("rowb") + lax.axis_index("rowb")
    place = place.astype(jnp.int32).reshape(1)
    rows = levels * width + nrhs
    counts = [rows - level * width for level in range(levels)]
    spread = inner_bits >= 3 and levels >= 4
    plan = None
    if spread:
        plan = Plan(counts[1], sum(counts[2:]) - width)
    square = (width, width)
    middle = up(width // 2, STEP)
    key, rest, scaled, lower = call(
        functools.partial(leaf_kernel, levels, width, blocks),
        [square, (sum(counts) - width, width), (blocks, rows, width), (blocks, max(blocks - 1, 1)) + square],
        ranks,
        place,
        right_side.T,
        leaves,
        bases,
        smem=2,
        hbm=2,
        scratch=[
            pltpu.VMEM((blocks, rows, width), F32),
            pltpu.VMEM((leaf_rows, leaf_rows), F32),
            pltpu.VMEM((levels, leaf_rows, width), F32),
            pltpu.SemaphoreType.DMA((blocks + 1,)),
        ],
    )
    coefs = []
    mine = send = None
    for level in range(levels - 1):
        count = counts[level] - width
        below = levels - 1 - level
        other_key = partner(key, level, inner_bits)
        scatter = spread and level == 1
        gather = spread and level == 2
        if scatter:
            near = partner(mine, level, inner_bits)
            send, other_key = lax.optimization_barrier((send, other_key))
            far = partner(send, level, inner_bits)
        elif gather:
            other_quarter = partner(quarter, level, inner_bits)
        else:
            other_rest = partner(rest, level, inner_bits)
        if scatter or gather:
            (half,) = call(functools.partial(pivot_kernel, 0, middle), [square], key, other_key)
            if scatter:
                half, near = lax.optimization_barrier((half, near))
                take = functools.partial(take_halves, plan)
                pieces = [place, rest, near, flip(near, 1)]
            else:
                half, other_quarter = lax.optimization_barrier((half, other_quarter))
                (quarter,) = call(add_kernel, [quarter.shape], quarter, other_quarter)
                take = functools.partial(take_quarters, plan)
                pieces = [place, quarter] + [flip(quarter, mask) for mask in (1, 2, 3)]
            (inv,) = call(functools.partial(pivot_kernel, middle, width), [square], half)
        else:
            (inv,) = call(functools.partial(pivot_kernel, 0, width), [square], key, other_key)
            take = take_full
            pieces = [rest, other_rest]
        total, coef, key = call(
            functools.partial(near_update, width, count, take),
            [(plan.far if gather else counts[level], width), (count, width), square],
            *pieces,
            inv,
            smem=1 if scatter or gather else 0,
        )
        coefs.append(coef)
        if scatter:
            (quarter,) = call(
                functools.partial(quarter_update, plan, width, count, below),
                [(plan.quarter, width)],
                place,
                total,
                coef,
                rest,
                far,
                smem=1,
                scratch=[pltpu.VMEM((plan.far, width), F32)],
            )
            continue
        next_scatter = spread and level == 0
        shapes = [(sum(counts[level + 1 :]) - width, width)]
        if next_scatter:
            shapes += [(plan.half, width), (plan.quarter, width)]
        rest, *sent = call(
            functools.partial(far_update, plan, width, count, below, next_scatter),
            shapes,
            place,
            total,
            coef,
            *([] if gather else [rest, other_rest]),
            smem=1,
        )
        if next_scatter:
            mine, send = sent
    last = jnp.concatenate([key, rest], axis=0)
    other_last = partner(last, levels - 1, inner_bits)
    (weights,) = call(
        functools.partial(back_kernel, width, blocks), [(rows, leaf_rows)], scaled, lower
    )
    (result,) = call(
        functools.partial(final_kernel, levels, width),
        [(nrhs, leaf_rows)],
        last,
        other_last,
        weights,
        *coefs,
    )
    return result.T


def solution(mesh):
    placed = (
        P(("rowa", "rowb"), None),
        P(("rowa", "rowb"), None),
        P(None, ("rowa", "rowb"), None),
        P(),
    )
    return jax.shard_map(
        body, mesh=mesh, in_specs=placed, out_specs=P(("rowa", "rowb"), None), check_vma=False
    )
```

```python
import functools

import jax
import jax.numpy as jnp
from jax import lax
from jax.experimental import pallas as pl
from jax.experimental.pallas import tpu as pltpu
from jax.sharding import PartitionSpec as P

F32 = jnp.float32
BF16 = jnp.bfloat16
STEP = 16
VMEM_LIMIT = 48 * 1024 * 1024


def split3(value):
    high = value.astype(BF16)
    rest = value - high.astype(F32)
    middle = rest.astype(BF16)
    return high, middle, (rest - middle.astype(F32)).astype(BF16)


def left6(value):
    high, middle, low = split3(value)
    return jnp.concatenate([high, high, middle, high, middle, low], axis=1)


def right6(value, axis):
    high, middle, low = split3(value)
    return jnp.concatenate([high, middle, high, low, middle, high], axis=axis)


def pad_rows(value):
    extra = -value.shape[0] % 16
    if not extra:
        return value
    return jnp.concatenate([value, jnp.zeros((extra, value.shape[1]), value.dtype)], axis=0)


def dot(left, right):
    product = jnp.dot(left6(pad_rows(left)), right6(right, 0), preferred_element_type=F32)
    return product[: left.shape[0]]


def dot_nt(left, right):
    product = dot6_nt(left6(pad_rows(left)), right6(right, 1))
    return product[: left.shape[0]]


def dot6_nt(left, right):
    return lax.dot_general(left, right, (((1,), (1,)), ((), ())), preferred_element_type=F32)


def spread_row(value, index):
    return jnp.broadcast_to(value[index : index + 1, :], value.shape)


def eliminate(panel, pivots):
    sub = lax.broadcasted_iota(jnp.int32, panel[0].shape, 0)
    pieces = range(len(panel))
    pivot = spread_row(pivots[0][0], 0)
    for step in range(STEP):
        piece, index = divmod(step, 8)
        scale = pltpu.reciprocal(pivot, approx=True)
        if step + 1 < STEP:
            next_piece, next_index = divmod(step + 1, 8)
            cross = spread_row(pivots[step][next_piece], next_index) * spread_row(
                pivots[step + 1][piece], index
            )
            pivot = spread_row(pivots[step + 1][next_piece], next_index) - cross * scale
        own = sub == index
        factors = [
            (jnp.where(own, -1.0, pivots[step][at]) if at == piece else pivots[step][at]) * scale
            for at in pieces
        ]

        def reduce(column):
            row = spread_row(column[piece], index)
            return [
                (jnp.where(own, 0.0, column[at]) if at == piece else column[at]) - factors[at] * row
                for at in pieces
            ]

        panel = reduce(panel)
        for later in range(step + 1, STEP):
            pivots[later] = reduce(pivots[later])
    return panel


def sweep(matrix, first, last, tick=lambda: None):
    size = matrix.shape[0]
    pieces = range(STEP // 8)
    lane = lax.broadcasted_iota(jnp.int32, (8, size), 1)
    sub = lax.broadcasted_iota(jnp.int32, (8, size), 0)
    lane_all = lax.broadcasted_iota(jnp.int32, (size, size), 1)
    sub_all = lax.broadcasted_iota(jnp.int32, (size, size), 0)
    rows = [matrix[first + 8 * at : first + 8 * at + 8] for at in pieces]
    for start in range(first, last, STEP):
        stop = start + STEP
        more = stop < size
        pivots = [
            [jnp.broadcast_to(rows[at][:, start + index : start + index + 1], (8, size)) for at in pieces]
            for index in range(STEP)
        ]
        inside = (lane >= start) & (lane < stop)
        panel = [
            jnp.where(inside, jnp.where(lane - start == sub + 8 * at, 1.0, 0.0), rows[at])
            for at in pieces
        ]
        row_inside = (sub_all >= start) & (sub_all < stop)
        lane_inside = (lane_all >= start) & (lane_all < stop)
        column = jnp.where(row_inside, 0.0, matrix)[:, start:stop]
        base = jnp.where(row_inside | lane_inside, 0.0, matrix)
        following = []
        if more:
            following = [matrix[stop + 8 * at : stop + 8 * at + 8] for at in pieces]
        ahead = [
            [jnp.broadcast_to(piece[:, start + index : start + index + 1], (8, size)) for piece in following]
            for index in range(STEP)
        ]
        tick()
        panel = eliminate(panel, pivots)
        if more:
            rows = []
            for at in pieces:
                terms = [
                    ahead[index][at] * spread_row(panel[index // 8], index % 8)
                    for index in range(STEP)
                ]
                while len(terms) > 1:
                    terms = [terms[at2] + terms[at2 + 1] for at2 in range(0, len(terms), 2)]
                rows.append(base[stop + 8 * at : stop + 8 * at + 8] - terms[0])
        joined = jnp.concatenate(panel, axis=0)
        matrix = base - jnp.dot(left6(column), right6(joined, 0), preferred_element_type=F32)
        parts = [matrix[:start]] if start else []
        parts.append(joined)
        if more:
            parts += rows
        if stop + (STEP if more else 0) < size:
            parts.append(matrix[stop + STEP :])
        matrix = jnp.concatenate(parts, axis=0)
    return matrix


def inverse(matrix, tick=lambda: None):
    return sweep(matrix, 0, matrix.shape[0], tick)


def add_eye(matrix):
    row = lax.broadcasted_iota(jnp.int32, matrix.shape, 0)
    column = lax.broadcasted_iota(jnp.int32, matrix.shape, 1)
    return matrix + jnp.where(row == column, 1.0, 0.0)


def leaf_kernel(levels, width, blocks, ranks_ref, place_ref, rhs_ref, leaf_hbm, bases_hbm, *refs):
    key_ref, rest_ref, scaled_ref, lower_ref, v_ref, v6_ref, s6_ref, leaf_ref, bases_ref, sem = refs
    nrhs = rhs_ref.shape[0]
    place = place_ref[0]
    rows = levels * width
    count = rows + nrhs
    padded = v6_ref.shape[0]
    spans = [slice(block * width, (block + 1) * width) for block in range(blocks)]
    leaf_copies = [
        pltpu.make_async_copy(leaf_hbm.at[span], leaf_ref.at[span], sem.at[index])
        for index, span in enumerate(spans)
    ]
    bases_copy = pltpu.make_async_copy(bases_hbm, bases_ref, sem.at[blocks])
    for copy in leaf_copies:
        copy.start()
    bases_copy.start()

    tasks = []
    quota = [0]

    def tick():
        for _ in range(min(quota[0], len(tasks))):
            tasks.pop(0)()

    def run(steps):
        quota[0] = -(-len(tasks) // steps)

    def arrive():
        for copy in leaf_copies[1:]:
            copy.wait()
        bases_copy.wait()

    def load(block, level):
        sub = lax.broadcasted_iota(jnp.int32, (width, width), 0)
        rank = ranks_ref[2 ** (levels - level) + lax.shift_right_logical(place, level) - 1]
        piece = jnp.where(sub < rank, bases_ref[level - 1, spans[block], :].T, 0.0)
        span = slice((level - 1) * width, level * width)
        v_ref[block, span, :] = piece
        if block == 0:
            v6_ref[span, :] = left6(piece)

    def load_rhs():
        for block, span in enumerate(spans):
            piece = rhs_ref[:, span]
            piece = jnp.concatenate([piece, jnp.zeros((padded - count, width), F32)], axis=0)
            v_ref[block, rows:padded, :] = piece
            if block == 0:
                v6_ref[rows:padded, :] = left6(piece)

    chunk = up(padded // 3, 16)
    chunks = [slice(at, min(at + chunk, padded)) for at in range(0, padded, chunk)]

    def split_values(block, span):
        v6_ref[span, :] = left6(v_ref[block, span, :])

    def apply(block, weights, span):
        product = jnp.dot(v6_ref[span, :], weights, preferred_element_type=F32)
        scaled = product[:, :width]
        scaled_ref[block, span, :] = scaled
        stop = min(span.stop, rows)
        if span.start < stop:
            s6_ref[span.start : stop, :] = right6(scaled[: stop - span.start], 1)
        for later in range(block + 1, blocks):
            at = (later - block) * width
            v_ref[later, span, :] = v_ref[later, span, :] - product[:, at : at + width]

    def store(block, target, span, value):
        target[span, :] = value if block == 0 else target[span, :] + value

    def gram(block, level):
        low = level * width
        pair = min(2, levels - level)
        product = dot6_nt(v6_ref[low:, :], s6_ref[low : low + pair * width, :])
        for index in range(pair):
            value = product[index * width : count - low, index * width : (index + 1) * width]
            offset = sum(count - done * width for done in range(level + index)) - width
            if offset < 0:
                store(block, key_ref, slice(0, width), value[:width])
                value = value[width:]
                offset = 0
            store(block, rest_ref, slice(offset, offset + value.shape[0]), value)

    leaf_copies[0].wait()
    tasks.append(arrive)
    tasks += [functools.partial(load, 0, level) for level in range(1, levels + 1)]
    tasks.append(load_rhs)
    for block in range(1, blocks):
        tasks += [functools.partial(load, block, level) for level in range(1, levels + 1)]
    schur = {(0, 0): leaf_ref[spans[0], spans[0]]}
    for block in range(blocks):
        run(width // STEP)
        inv = inverse(schur[block, block], tick)
        while tasks:
            tasks.pop(0)()
        if block == 0:
            for first in range(blocks):
                for second in range(blocks):
                    if first or second:
                        schur[first, second] = leaf_ref[spans[first], spans[second]]
        rest = range(block + 1, blocks)
        weights = right6(inv, 0)
        if rest:
            right = jnp.concatenate([schur[block, later] for later in rest], axis=1)
            upper = dot(inv, right)
            split = right6(upper, 0)
            for index, later in enumerate(rest):
                lower_ref[block, later - 1] = upper[:, index * width : (index + 1) * width]

            def reduce(first, block=block, rest=rest, split=split):
                product = jnp.dot(left6(schur[first, block]), split, preferred_element_type=F32)
                for index, later in enumerate(rest):
                    at = slice(index * width, (index + 1) * width)
                    schur[first, later] = schur[first, later] - product[:, at]

            reduce(block + 1)
            tasks += [functools.partial(reduce, first) for first in rest[1:]]
            weights = jnp.concatenate([weights, split], axis=1)
        if block:
            tasks += [functools.partial(split_values, block, span) for span in chunks]
        tasks += [functools.partial(apply, block, weights, span) for span in chunks]
        tasks += [functools.partial(gram, block, level) for level in range(0, levels, 2)]
    while tasks:
        tasks.pop(0)()


def pivot_kernel(first, last, *refs):
    if first == 0:
        matrix = add_eye(refs[0][...] + refs[1][...])
    else:
        matrix = refs[0][...]
    refs[-1][...] = sweep(matrix, first, last)


def near_update(width, count, take, *refs):
    rest_ref, coef_ref, key_ref = refs[-3:]
    inv_ref = refs[-4]
    take(refs[:-4], rest_ref)
    rest = rest_ref[:count]
    coef_ref[...] = dot(rest, inv_ref[...])
    key_ref[...] = rest_ref[count : count + width] - dot_nt(coef_ref[:width], rest_ref[:width])


def take_full(refs, rest_ref):
    own_ref, other_ref = refs
    rows = rest_ref.shape[0]
    rest_ref[...] = own_ref[:rows] + other_ref[:rows]


def take_halves(plan, refs, rest_ref):
    place_ref, own_ref, near_ref, cross_ref = refs
    side = place_ref[0] & 1
    for index, source in ((side, near_ref), (side ^ 1, cross_ref)):
        span = pl.ds(plan.half_at(index), plan.half)
        rest_ref[span, :] = own_ref[span, :] + source[...]


def take_quarters(plan, refs, rest_ref):
    for index, source in enumerate(refs[1:]):
        span = pl.ds(plan.quarter_at((refs[0][0] & 3) ^ index), plan.quarter)
        rest_ref[span, :] = source[...]


def rank_update(width, count, below, rest_ref, coef_ref, put):
    offset = 0
    for level in range(below):
        low = level * width
        start = low + width if level == 0 else low
        if start < count:
            put(offset, dot_nt(coef_ref[start:, :], rest_ref[low : low + width, :]))
        offset += count - start


def far_update(plan, width, count, below, scatter, *refs):
    place_ref, rest_ref, coef_ref, *more = refs
    outs = more[-3:] if scatter else more[-1:]
    pair = more[: -len(outs)]
    skip = count + width

    def put(offset, product):
        span = slice(skip + offset, skip + offset + product.shape[0])
        if pair:
            value = pair[0][span, :] + pair[1][span, :]
        else:
            value = rest_ref[span, :]
        outs[0][offset : offset + product.shape[0], :] = value - product

    rank_update(width, count, below, rest_ref, coef_ref, put)
    if scatter:
        place = place_ref[0]
        outs[1][...] = outs[0][pl.ds(plan.half_at(place & 1), plan.half), :]
        outs[2][...] = outs[0][
            pl.ds(plan.near + plan.quarter_at((place & 3) ^ 2), plan.quarter), :
        ]


def quarter_update(plan, width, count, below, *refs):
    place_ref, rest_ref, coef_ref, own_ref, other_ref, out_ref, product_ref = refs

    def put(offset, product):
        product_ref[offset : offset + product.shape[0], :] = product

    rank_update(width, count, below, rest_ref, coef_ref, put)
    at = plan.quarter_at(place_ref[0] & 3)
    out_ref[...] = (
        own_ref[pl.ds(plan.near + at, plan.quarter), :]
        + other_ref[...]
        - product_ref[pl.ds(at, plan.quarter), :]
    )


def add_kernel(own_ref, other_ref, out_ref):
    out_ref[...] = own_ref[...] + other_ref[...]


def back_kernel(width, blocks, scaled_ref, lower_ref, out_ref):
    values = [None] * blocks
    for block in reversed(range(blocks)):
        value = scaled_ref[block]
        for later in range(block + 1, blocks):
            value = value - dot_nt(values[later], lower_ref[block, later - 1])
        values[block] = value
        out_ref[:, block * width : (block + 1) * width] = value


def final_kernel(levels, width, own_ref, other_ref, weights_ref, *refs):
    coef_refs, out_ref = refs[:-1], refs[-1]
    inv = inverse(add_eye(own_ref[:width] + other_ref[:width]))
    known = [dot(own_ref[width:] + other_ref[width:], inv)]
    for level in reversed(range(levels - 1)):
        coef = coef_refs[level]
        count = (levels - 1 - level) * width
        value = coef[count:, :]
        for index, later in enumerate(known):
            low = (len(known) - 1 - index) * width
            value = value - dot(later, coef[low : low + width, :])
        known.append(value)
    rows = levels * width
    result = weights_ref[rows : rows + known[0].shape[0], :]
    for level in range(levels):
        result = result - dot(
            known[levels - 1 - level], weights_ref[level * width : (level + 1) * width, :]
        )
    out_ref[...] = result


def call(kernel, shapes, *operands, flops=0, smem=0, hbm=0, scratch=()):
    flops = flops or 2 * 10**9
    space = [pl.BlockSpec(memory_space=pltpu.SMEM)] * smem
    space += [pl.BlockSpec(memory_space=pltpu.VMEM)] * (len(operands) - smem - hbm)
    space += [pl.BlockSpec(memory_space=pltpu.HBM)] * hbm
    outs = [jax.ShapeDtypeStruct(shape, F32) for shape in shapes]
    return pl.pallas_call(
        kernel,
        out_shape=outs,
        in_specs=space,
        out_specs=[pl.BlockSpec(memory_space=pltpu.VMEM)] * len(outs),
        scratch_shapes=list(scratch),
        compiler_params=pltpu.CompilerParams(vmem_limit_bytes=VMEM_LIMIT),
        cost_estimate=pl.CostEstimate(flops=flops, bytes_accessed=flops // 300, transcendentals=0),
    )(*operands)


def flip(value, mask, axis="rowb"):
    pairs = [(source, source ^ mask) for source in range(lax.axis_size(axis))]
    return lax.ppermute(value, axis, pairs)


def partner(value, level, inner_bits):
    if level < inner_bits:
        return flip(value, 2**level)
    return flip(value, 2 ** (level - inner_bits), "rowa")


def up(value, step):
    return -(-value // step) * step


class Plan:
    def __init__(self, near, far):
        self.near, self.far = near, far
        self.half = up(near, 16) // 2
        self.quarter = up(far, 32) // 4

    def half_at(self, side):
        return pl.multiple_of(side * (self.near - self.half), 8)

    def quarter_at(self, index):
        return pl.multiple_of(jnp.minimum(index * self.quarter, self.far - self.quarter), 8)


def body(right_side, leaves, bases, ranks):
    levels = bases.shape[0]
    leaf_rows = leaves.shape[0]
    width = bases.shape[2]
    nrhs = right_side.shape[1]
    blocks = leaf_rows // width
    inner_bits = lax.axis_size("rowb").bit_length() - 1
    place = lax.axis_index("rowa") * lax.axis_size("rowb") + lax.axis_index("rowb")
    place = place.astype(jnp.int32).reshape(1)
    rows = levels * width + nrhs
    padded = up(rows, 16)
    counts = [rows - level * width for level in range(levels)]
    spread = inner_bits >= 3 and levels >= 4
    plan = None
    if spread:
        plan = Plan(counts[1], sum(counts[2:]) - width)
    square = (width, width)
    middle = up(width // 2, STEP)
    key, rest, scaled, lower = call(
        functools.partial(leaf_kernel, levels, width, blocks),
        [
            square,
            (sum(counts) - width, width),
            (blocks, padded, width),
            (blocks, max(blocks - 1, 1)) + square,
        ],
        ranks,
        place,
        right_side.T,
        leaves,
        bases,
        smem=2,
        hbm=2,
        scratch=[
            pltpu.VMEM((blocks, padded, width), F32),
            pltpu.VMEM((padded, 6 * width), BF16),
            pltpu.VMEM((levels * width, 6 * width), BF16),
            pltpu.VMEM((leaf_rows, leaf_rows), F32),
            pltpu.VMEM((levels, leaf_rows, width), F32),
            pltpu.SemaphoreType.DMA((blocks + 1,)),
        ],
    )
    coefs = []
    mine = send = None
    for level in range(levels - 1):
        count = counts[level] - width
        below = levels - 1 - level
        other_key = partner(key, level, inner_bits)
        scatter = spread and level == 1
        gather = spread and level == 2
        if scatter:
            near = partner(mine, level, inner_bits)
            send, other_key = lax.optimization_barrier((send, other_key))
            far = partner(send, level, inner_bits)
        elif gather:
            other_quarter = partner(quarter, level, inner_bits)
        else:
            other_rest = partner(rest, level, inner_bits)
        if scatter or gather:
            (half,) = call(functools.partial(pivot_kernel, 0, middle), [square], key, other_key)
            if scatter:
                half, near = lax.optimization_barrier((half, near))
                take = functools.partial(take_halves, plan)
                pieces = [place, rest, near, flip(near, 1)]
            else:
                half, other_quarter = lax.optimization_barrier((half, other_quarter))
                (quarter,) = call(add_kernel, [quarter.shape], quarter, other_quarter)
                take = functools.partial(take_quarters, plan)
                pieces = [place, quarter] + [flip(quarter, mask) for mask in (1, 2, 3)]
            (inv,) = call(functools.partial(pivot_kernel, middle, width), [square], half)
        else:
            (inv,) = call(functools.partial(pivot_kernel, 0, width), [square], key, other_key)
            take = take_full
            pieces = [rest, other_rest]
        total, coef, key = call(
            functools.partial(near_update, width, count, take),
            [(plan.far if gather else counts[level], width), (count, width), square],
            *pieces,
            inv,
            smem=1 if scatter or gather else 0,
        )
        coefs.append(coef)
        if scatter:
            (quarter,) = call(
                functools.partial(quarter_update, plan, width, count, below),
                [(plan.quarter, width)],
                place,
                total,
                coef,
                rest,
                far,
                smem=1,
                scratch=[pltpu.VMEM((plan.far, width), F32)],
            )
            continue
        next_scatter = spread and level == 0
        shapes = [(sum(counts[level + 1 :]) - width, width)]
        if next_scatter:
            shapes += [(plan.half, width), (plan.quarter, width)]
        rest, *sent = call(
            functools.partial(far_update, plan, width, count, below, next_scatter),
            shapes,
            place,
            total,
            coef,
            *([] if gather else [rest, other_rest]),
            smem=1,
        )
        if next_scatter:
            mine, send = sent
    last = jnp.concatenate([key, rest], axis=0)
    other_last = partner(last, levels - 1, inner_bits)
    (weights,) = call(
        functools.partial(back_kernel, width, blocks), [(padded, leaf_rows)], scaled, lower
    )
    (result,) = call(
        functools.partial(final_kernel, levels, width),
        [(nrhs, leaf_rows)],
        last,
        other_last,
        weights,
        *coefs,
    )
    return result.T


def solution(mesh):
    placed = (
        P(("rowa", "rowb"), None),
        P(("rowa", "rowb"), None),
        P(None, ("rowa", "rowb"), None),
        P(),
    )
    return jax.shard_map(
        body, mesh=mesh, in_specs=placed, out_specs=P(("rowa", "rowb"), None), check_vma=False
    )
```

```python
import functools

import jax
import jax.numpy as jnp
from jax import lax
from jax.experimental import pallas as pl
from jax.experimental.pallas import tpu as pltpu
from jax.sharding import PartitionSpec as P

F32 = jnp.float32
BF16 = jnp.bfloat16
STEP = 16
VMEM_LIMIT = 48 * 1024 * 1024
LEAF_LIMIT = 48 * 1024 * 1024


def split3(value):
    high = value.astype(BF16)
    rest = value - high.astype(F32)
    middle = rest.astype(BF16)
    return high, middle, (rest - middle.astype(F32)).astype(BF16)


def left6(value):
    high, middle, low = split3(value)
    return jnp.concatenate([high, high, middle, high, middle, low], axis=1)


def right6(value, axis):
    high, middle, low = split3(value)
    return jnp.concatenate([high, middle, high, low, middle, high], axis=axis)


def pad_rows(value):
    extra = -value.shape[0] % 16
    if not extra:
        return value
    return jnp.concatenate([value, jnp.zeros((extra, value.shape[1]), value.dtype)], axis=0)


def dot(left, right):
    product = jnp.dot(left6(pad_rows(left)), right6(right, 0), preferred_element_type=F32)
    return product[: left.shape[0]]


def dot_nt(left, right):
    product = dot6_nt(left6(pad_rows(left)), right6(right, 1))
    return product[: left.shape[0]]


def dot6_nt(left, right):
    return lax.dot_general(left, right, (((1,), (1,)), ((), ())), preferred_element_type=F32)


def spread_row(value, index):
    return jnp.broadcast_to(value[index : index + 1, :], value.shape)


def eliminate(panel, pivots):
    sub = lax.broadcasted_iota(jnp.int32, panel[0].shape, 0)
    pieces = range(len(panel))
    pivot = spread_row(pivots[0][0], 0)
    for step in range(STEP):
        piece, index = divmod(step, 8)
        scale = pltpu.reciprocal(pivot, approx=True)
        if step + 1 < STEP:
            next_piece, next_index = divmod(step + 1, 8)
            cross = spread_row(pivots[step][next_piece], next_index) * spread_row(
                pivots[step + 1][piece], index
            )
            pivot = spread_row(pivots[step + 1][next_piece], next_index) - cross * scale
        own = sub == index
        factors = [
            (jnp.where(own, -1.0, pivots[step][at]) if at == piece else pivots[step][at]) * scale
            for at in pieces
        ]

        def reduce(column):
            row = spread_row(column[piece], index)
            return [
                (jnp.where(own, 0.0, column[at]) if at == piece else column[at]) - factors[at] * row
                for at in pieces
            ]

        panel = reduce(panel)
        for later in range(step + 1, STEP):
            pivots[later] = reduce(pivots[later])
    return panel


def sweep(matrix, first, last, tick=lambda: None):
    size = matrix.shape[0]
    pieces = range(STEP // 8)
    lane = lax.broadcasted_iota(jnp.int32, (8, size), 1)
    sub = lax.broadcasted_iota(jnp.int32, (8, size), 0)
    lane_all = lax.broadcasted_iota(jnp.int32, (size, size), 1)
    sub_all = lax.broadcasted_iota(jnp.int32, (size, size), 0)
    rows = [matrix[first + 8 * at : first + 8 * at + 8] for at in pieces]
    for start in range(first, last, STEP):
        stop = start + STEP
        more = stop < size
        pivots = [
            [jnp.broadcast_to(rows[at][:, start + index : start + index + 1], (8, size)) for at in pieces]
            for index in range(STEP)
        ]
        inside = (lane >= start) & (lane < stop)
        panel = [
            jnp.where(inside, jnp.where(lane - start == sub + 8 * at, 1.0, 0.0), rows[at])
            for at in pieces
        ]
        row_inside = (sub_all >= start) & (sub_all < stop)
        lane_inside = (lane_all >= start) & (lane_all < stop)
        column = jnp.where(row_inside, 0.0, matrix)[:, start:stop]
        base = jnp.where(row_inside | lane_inside, 0.0, matrix)
        following = []
        if more:
            following = [matrix[stop + 8 * at : stop + 8 * at + 8] for at in pieces]
        ahead = [
            [jnp.broadcast_to(piece[:, start + index : start + index + 1], (8, size)) for piece in following]
            for index in range(STEP)
        ]
        tick()
        panel = eliminate(panel, pivots)
        if more:
            rows = []
            for at in pieces:
                terms = [
                    ahead[index][at] * spread_row(panel[index // 8], index % 8)
                    for index in range(STEP)
                ]
                while len(terms) > 1:
                    terms = [terms[at2] + terms[at2 + 1] for at2 in range(0, len(terms), 2)]
                rows.append(base[stop + 8 * at : stop + 8 * at + 8] - terms[0])
        joined = jnp.concatenate(panel, axis=0)
        matrix = base - jnp.dot(left6(column), right6(joined, 0), preferred_element_type=F32)
        parts = [matrix[:start]] if start else []
        parts.append(joined)
        if more:
            parts += rows
        if stop + (STEP if more else 0) < size:
            parts.append(matrix[stop + STEP :])
        matrix = jnp.concatenate(parts, axis=0)
    return matrix


def inverse(matrix, tick=lambda: None):
    return sweep(matrix, 0, matrix.shape[0], tick)


def add_eye(matrix):
    row = lax.broadcasted_iota(jnp.int32, matrix.shape, 0)
    column = lax.broadcasted_iota(jnp.int32, matrix.shape, 1)
    return matrix + jnp.where(row == column, 1.0, 0.0)


def gram_pair(levels, width, count, level, v6_ref, s6_ref):
    low = level * width
    pair = min(2, levels - level)
    product = dot6_nt(v6_ref[low:, :], s6_ref[low : low + pair * width, :])
    result = []
    for index in range(pair):
        value = product[index * width : count - low, index * width : (index + 1) * width]
        offset = sum(count - done * width for done in range(level + index)) - width
        if offset < 0:
            result.append((offset, value[:width]))
            value = value[width:]
            offset = 0
        result.append((offset, value))
    return result


def leaf_kernel(levels, width, blocks, ranks_ref, place_ref, rhs_hbm, leaf_hbm, bases_hbm, *refs):
    key_ref, rest_ref, scaled_ref, lower_ref, v6_ref, s6_ref, v_ref, *refs = refs
    rhs_ref, leaf_ref, bases_ref, sem = refs
    nrhs = rhs_ref.shape[0]
    place = place_ref[0]
    rows = levels * width
    count = rows + nrhs
    padded = v6_ref.shape[0]
    spans = [slice(block * width, (block + 1) * width) for block in range(blocks)]
    leaf_copies = [
        pltpu.make_async_copy(leaf_hbm.at[span], leaf_ref.at[span], sem.at[index])
        for index, span in enumerate(spans)
    ]
    other_copies = [
        pltpu.make_async_copy(bases_hbm, bases_ref, sem.at[blocks]),
        pltpu.make_async_copy(rhs_hbm, rhs_ref, sem.at[blocks + 1]),
    ]
    for copy in leaf_copies + other_copies:
        copy.start()

    tasks = []
    quota = [0]

    def tick():
        for _ in range(min(quota[0], len(tasks))):
            tasks.pop(0)()

    def run(steps):
        quota[0] = -(-len(tasks) // steps)

    def arrive():
        for copy in leaf_copies[1:] + other_copies:
            copy.wait()

    def load(block, level):
        sub = lax.broadcasted_iota(jnp.int32, (width, width), 0)
        rank = ranks_ref[2 ** (levels - level) + lax.shift_right_logical(place, level) - 1]
        piece = jnp.where(sub < rank, bases_ref[level - 1, spans[block], :].T, 0.0)
        span = slice((level - 1) * width, level * width)
        v_ref[block, span, :] = piece
        if block == 0:
            v6_ref[span, :] = left6(piece)

    def load_rhs():
        for block, span in enumerate(spans):
            piece = rhs_ref[:, span]
            piece = jnp.concatenate([piece, jnp.zeros((padded - count, width), F32)], axis=0)
            v_ref[block, rows:padded, :] = piece
            if block == 0:
                v6_ref[rows:padded, :] = left6(piece)

    chunk = up(padded // 3, 16)
    chunks = [slice(at, min(at + chunk, padded)) for at in range(0, padded, chunk)]

    def split_values(block, span):
        v6_ref[span, :] = left6(v_ref[block, span, :])

    def apply(block, weights, span):
        product = jnp.dot(v6_ref[span, :], weights, preferred_element_type=F32)
        scaled = product[:, :width]
        scaled_ref[block, span, :] = scaled
        stop = min(span.stop, rows)
        if span.start < stop:
            s6_ref[span.start : stop, :] = right6(scaled[: stop - span.start], 1)
        for later in range(block + 1, blocks):
            at = (later - block) * width
            v_ref[later, span, :] = v_ref[later, span, :] - product[:, at : at + width]

    def gram(block, level):
        for offset, value in gram_pair(levels, width, count, level, v6_ref, s6_ref):
            target = key_ref if offset < 0 else rest_ref
            span = slice(max(offset, 0), max(offset, 0) + value.shape[0])
            target[span, :] = value if block == 0 else target[span, :] + value

    leaf_copies[0].wait()
    tasks.append(arrive)
    tasks += [functools.partial(load, 0, level) for level in range(1, levels + 1)]
    tasks.append(load_rhs)
    for block in range(1, blocks):
        tasks += [functools.partial(load, block, level) for level in range(1, levels + 1)]
    schur = {(0, 0): leaf_ref[spans[0], spans[0]]}
    for block in range(blocks):
        run(width // STEP)
        inv = inverse(schur[block, block], tick)
        while tasks:
            tasks.pop(0)()
        if block == 0:
            for first in range(blocks):
                for second in range(blocks):
                    if first or second:
                        schur[first, second] = leaf_ref[spans[first], spans[second]]
        rest = range(block + 1, blocks)
        weights = right6(inv, 0)
        if rest:
            right = jnp.concatenate([schur[block, later] for later in rest], axis=1)
            upper = dot(inv, right)
            split = right6(upper, 0)
            for index, later in enumerate(rest):
                lower_ref[block, later - 1] = upper[:, index * width : (index + 1) * width]

            def reduce(first, block=block, rest=rest, split=split):
                product = jnp.dot(left6(schur[first, block]), split, preferred_element_type=F32)
                for index, later in enumerate(rest):
                    at = slice(index * width, (index + 1) * width)
                    schur[first, later] = schur[first, later] - product[:, at]

            reduce(block + 1)
            tasks += [functools.partial(reduce, first) for first in rest[1:]]
            weights = jnp.concatenate([weights, split], axis=1)
        if block:
            tasks += [functools.partial(split_values, block, span) for span in chunks]
        tasks += [functools.partial(apply, block, weights, span) for span in chunks]
        if block < blocks - 1:
            tasks += [functools.partial(gram, block, level) for level in range(0, levels, 2)]
    while tasks:
        tasks.pop(0)()
    key = dot6_nt(v6_ref[:width, :], s6_ref[:width, :])
    key_ref[...] = key_ref[...] + key if blocks > 1 else key
    if blocks == 1:
        rest_ref[...] = jnp.zeros_like(rest_ref)


def gram_kernel(levels, width, count, part_ref, v6_ref, s6_ref, rest_ref):
    for level in range(0, levels, 2):
        for offset, value in gram_pair(levels, width, count, level, v6_ref, s6_ref):
            if offset >= 0:
                span = slice(offset, offset + value.shape[0])
                rest_ref[span, :] = part_ref[span, :] + value


def pivot_kernel(first, last, *refs):
    if first == 0:
        matrix = add_eye(refs[0][...] + refs[1][...])
    else:
        matrix = refs[0][...]
    refs[-1][...] = sweep(matrix, first, last)


def near_update(width, count, take, *refs):
    rest_ref, coef_ref, key_ref = refs[-3:]
    inv_ref = refs[-4]
    take(refs[:-4], rest_ref)
    coef_ref[...] = dot(rest_ref[:count], inv_ref[...])
    next_key(width, count, rest_ref, coef_ref, key_ref)


def next_key(width, count, rest_ref, coef_ref, key_ref):
    key_ref[...] = rest_ref[count : count + width] - dot_nt(coef_ref[:width], rest_ref[:width])


def take_full(refs, rest_ref):
    own_ref, other_ref = refs
    rows = rest_ref.shape[0]
    rest_ref[...] = own_ref[:rows] + other_ref[:rows]


def take_halves(plan, refs, rest_ref):
    place_ref, own_ref, near_ref, cross_ref = refs
    side = place_ref[0] & 1
    for index, source in ((side, near_ref), (side ^ 1, cross_ref)):
        span = pl.ds(plan.near2_at(index), plan.near2)
        rest_ref[span, :] = own_ref[span, :] + source[...]


def take_quarters(plan, refs, rest_ref):
    place_ref, joined_ref, cross_ref = refs
    for index in range(4):
        source, at = (joined_ref, cross_ref)[index & 1], (index // 2) * plan.near3
        span = pl.ds(plan.near3_at((place_ref[0] & 3) ^ index), plan.near3)
        rest_ref[span, :] = source[at : at + plan.near3, :]


def rank_update(width, count, below, first, last, rest_ref, coef_ref, put):
    offset = 0
    for level in range(below):
        low = level * width
        start = low + width if level == 0 else low
        size = count - start
        begin, end = max(first - offset, 0), min(last - offset, size)
        if begin < end:
            product = dot_nt(coef_ref[start + begin : start + end, :], rest_ref[low : low + width, :])
            put(offset + begin, product)
        offset += size


def far_update(width, count, below, own_ref, other_ref, rest_ref, coef_ref, out_ref):
    skip = count + width

    def put(offset, product):
        span = slice(skip + offset, skip + offset + product.shape[0])
        out_ref[offset : offset + product.shape[0], :] = own_ref[span, :] + other_ref[span, :] - product

    rank_update(width, count, below, 0, out_ref.shape[0], rest_ref, coef_ref, put)


def part_update(plan, width, count, below, first, place_ref, *refs):
    own_ref, other_ref, rest_ref, coef_ref, out_ref, send_ref = refs
    skip = count + width
    place = place_ref[0]

    def put(offset, product):
        span = slice(skip + offset, skip + offset + product.shape[0])
        at = offset - first
        out_ref[at : at + product.shape[0], :] = own_ref[span, :] + other_ref[span, :] - product

    rank_update(width, count, below, first, first + out_ref.shape[0], rest_ref, coef_ref, put)
    if first == 0:
        send_ref[...] = out_ref[pl.ds(plan.near2_at(place & 1), plan.near2), :]
    else:
        send_ref[: plan.near3, :] = out_ref[pl.ds(plan.near3_at((place & 3) ^ 2), plan.near3), :]
        send_ref[plan.near3 :, :] = out_ref[pl.ds(plan.rows3 + plan.far3_at(place & 1), plan.far3), :]


def quarter_update(plan, width, count, below, *refs):
    place_ref, own_ref, near_ref, cross_ref, far_own_ref, far_ref, inv_ref = refs[:7]
    rest_ref, coef_ref, out_ref, product_ref = refs[7:]
    take_halves(plan, (place_ref, own_ref, near_ref, cross_ref), rest_ref)
    coef_ref[...] = dot(rest_ref[:count], inv_ref[...])

    def put(offset, product):
        product_ref[offset : offset + product.shape[0], :] = product

    rank_update(width, count, below, 0, plan.rows3, rest_ref, coef_ref, put)
    span = pl.ds(plan.near3_at(place_ref[0] & 3), plan.near3)
    out_ref[...] = far_own_ref[span, :] + far_ref[: plan.near3, :] - product_ref[span, :]


def half_update(plan, width, count, below, *refs):
    place_ref, rest_ref, coef_ref, own_ref, far_ref, out_ref, product_ref = refs

    def put(offset, product):
        at = offset - plan.rows3
        product_ref[at : at + product.shape[0], :] = product

    rank_update(width, count, below, plan.rows3, plan.far, rest_ref, coef_ref, put)
    at = plan.far3_at(place_ref[0] & 1)
    out_ref[...] = (
        own_ref[pl.ds(plan.rows3 + at, plan.far3), :]
        + far_ref[plan.near3 :, :]
        - product_ref[pl.ds(at, plan.far3), :]
    )


def joined_update(plan, width, count, below, *refs):
    place_ref, half_ref, cross_ref, rest_ref, coef_ref, out_ref, total_ref = refs
    side = place_ref[0] & 1
    for index, source in ((side, half_ref), (side ^ 1, cross_ref)):
        total_ref[pl.ds(plan.far3_at(index), plan.far3), :] = source[...]

    def put(offset, product):
        span = slice(offset, offset + product.shape[0])
        out_ref[span, :] = total_ref[span, :] - product

    rank_update(width, count, below, 0, out_ref.shape[0], rest_ref, coef_ref, put)


def add_kernel(own_ref, other_ref, out_ref):
    out_ref[...] = own_ref[...] + other_ref[...]


def join_kernel(first_ref, second_ref, out_ref):
    rows = first_ref.shape[0]
    out_ref[:rows] = first_ref[...]
    out_ref[rows:] = second_ref[...]


def back_kernel(width, blocks, scaled_ref, lower_ref, out_ref):
    values = [None] * blocks
    for block in reversed(range(blocks)):
        value = scaled_ref[block]
        for later in range(block + 1, blocks):
            value = value - dot_nt(values[later], lower_ref[block, later - 1])
        values[block] = value
        out_ref[:, block * width : (block + 1) * width] = value


def fold_kernel(levels, width, nrhs, weights_ref, *refs):
    coef_refs, out_ref = refs[:-1], refs[-1]
    known = [None] * (levels - 1)
    for level in reversed(range(levels - 1)):
        coef = coef_refs[level]
        value = coef[(levels - 2 - level) * width :, :]
        above = range(level + 1, levels - 1)
        if above:
            value = value - dot(
                jnp.concatenate([known[later] for later in above], axis=1),
                coef[: len(above) * width, :],
            )
        known[level] = value
    low = (levels - 1) * width
    out_ref[...] = weights_ref[low : low + width + nrhs, :] - dot(
        jnp.concatenate(known, axis=1), weights_ref[:low, :]
    )


def final_kernel(width, own_ref, other_ref, folded_ref, out_ref):
    inv = inverse(add_eye(own_ref[:width] + other_ref[:width]))
    coef = dot(own_ref[width:] + other_ref[width:], inv)
    out_ref[...] = folded_ref[width:, :] - dot(coef, folded_ref[:width, :])


def call(kernel, shapes, *operands, cost=1.5, smem=0, hbm=0, scratch=(), limit=VMEM_LIMIT):
    flops = int(cost * 10**9)
    space = [pl.BlockSpec(memory_space=pltpu.SMEM)] * smem
    space += [pl.BlockSpec(memory_space=pltpu.VMEM)] * (len(operands) - smem - hbm)
    space += [pl.BlockSpec(memory_space=pltpu.HBM)] * hbm
    outs = [
        shape if isinstance(shape, jax.ShapeDtypeStruct) else jax.ShapeDtypeStruct(shape, F32)
        for shape in shapes
    ]
    return pl.pallas_call(
        kernel,
        out_shape=outs,
        in_specs=space,
        out_specs=[pl.BlockSpec(memory_space=pltpu.VMEM)] * len(outs),
        scratch_shapes=list(scratch),
        compiler_params=pltpu.CompilerParams(vmem_limit_bytes=limit),
        cost_estimate=pl.CostEstimate(flops=flops, bytes_accessed=flops // 300, transcendentals=0),
    )(*operands)


def flip(value, mask, axis="rowb"):
    pairs = [(source, source ^ mask) for source in range(lax.axis_size(axis))]
    return lax.ppermute(value, axis, pairs)


def partner(value, level, inner_bits):
    if level < inner_bits:
        return flip(value, 2**level)
    return flip(value, 2 ** (level - inner_bits), "rowa")


def up(value, step):
    return -(-value // step) * step


class Plan:
    def __init__(self, near, rows3, last3):
        self.near, self.rows3, self.last3, self.far = near, rows3, last3, rows3 + last3
        self.near2 = up(near, 16) // 2
        self.near3 = up(rows3, 32) // 4
        self.far3 = up(last3, 16) // 2

    def near2_at(self, side):
        return pl.multiple_of(side * (self.near - self.near2), 8)

    def near3_at(self, index):
        return pl.multiple_of(jnp.minimum(index * self.near3, self.rows3 - self.near3), 8)

    def far3_at(self, side):
        return pl.multiple_of(side * (self.last3 - self.far3), 8)


def body(right_side, leaves, bases, ranks):
    levels = bases.shape[0]
    leaf_rows = leaves.shape[0]
    width = bases.shape[2]
    nrhs = right_side.shape[1]
    blocks = leaf_rows // width
    inner_bits = lax.axis_size("rowb").bit_length() - 1
    place = lax.axis_index("rowa") * lax.axis_size("rowb") + lax.axis_index("rowb")
    place = place.astype(jnp.int32).reshape(1)
    rows = levels * width + nrhs
    padded = up(rows, 16)
    counts = [rows - level * width for level in range(levels)]
    spread = inner_bits >= 3 and levels >= 4
    plan = None
    if spread:
        plan = Plan(counts[1], counts[2], sum(counts[3:]) - width)
    square = (width, width)
    middle = up(width // 2, STEP)
    key, part, scaled, lower, values6, scaled6 = call(
        functools.partial(leaf_kernel, levels, width, blocks),
        [
            square,
            (sum(counts) - width, width),
            (blocks, padded, width),
            (blocks, max(blocks - 1, 1)) + square,
            jax.ShapeDtypeStruct((padded, 6 * width), BF16),
            jax.ShapeDtypeStruct((levels * width, 6 * width), BF16),
        ],
        ranks,
        place,
        *[pltpu.with_memory_space_constraint(each, pltpu.HBM) for each in (right_side.T, leaves, bases)],
        smem=2,
        hbm=3,
        limit=LEAF_LIMIT,
        scratch=[
            pltpu.VMEM((blocks, padded, width), F32),
            pltpu.VMEM((nrhs, leaf_rows), F32),
            pltpu.VMEM((leaf_rows, leaf_rows), F32),
            pltpu.VMEM((levels, leaf_rows, width), F32),
            pltpu.SemaphoreType.DMA((blocks + 2,)),
        ],
    )
    (rest,) = call(
        functools.partial(gram_kernel, levels, width, rows),
        [(sum(counts) - width, width)],
        part,
        values6,
        scaled6,
    )
    (weights,) = call(
        functools.partial(back_kernel, width, blocks), [(padded, leaf_rows)], scaled, lower
    )
    coefs = []
    for level in range(levels - 1):
        count = counts[level] - width
        below = levels - 1 - level
        following = sum(counts[level + 1 :]) - width
        if spread and level == 1:
            other_key = partner(key, level, inner_bits)
            near = partner(mine, level, inner_bits)
            far = partner(send, level, inner_bits)
            (half,) = call(functools.partial(pivot_kernel, 0, middle), [square], key, other_key)
            half, near = lax.optimization_barrier((half, near))
            cross = flip(near, 1)
            (inv,) = call(functools.partial(pivot_kernel, middle, width), [square], half)
            total, coef, quarter = call(
                functools.partial(quarter_update, plan, width, count, below),
                [(plan.near, width), (count, width), (plan.near3, width)],
                place,
                rest_near,
                near,
                cross,
                rest_far,
                far,
                inv,
                smem=1,
                scratch=[pltpu.VMEM((plan.rows3, width), F32)],
            )
            (key,) = call(functools.partial(next_key, width, count), [square], total, coef, cost=0.3)
            (last_half,) = call(
                functools.partial(half_update, plan, width, count, below),
                [(plan.far3, width)],
                place,
                total,
                coef,
                rest_far,
                far,
                smem=1,
                scratch=[pltpu.VMEM((plan.last3, width), F32)],
            )
        elif spread and level == 2:
            other_quarter = partner(quarter, level, inner_bits)
            other_key = partner(key, level, inner_bits)
            other_half = partner(last_half, level, inner_bits)
            quarter, weights = lax.optimization_barrier((quarter, weights))
            (quarter,) = call(add_kernel, [quarter.shape], quarter, other_quarter, cost=0.1)
            other_key, _ = lax.optimization_barrier((other_key, quarter))
            opposite = flip(quarter, 2)
            (half,) = call(functools.partial(pivot_kernel, 0, middle), [square], key, other_key)
            half, opposite = lax.optimization_barrier((half, opposite))
            (joined,) = call(join_kernel, [(2 * plan.near3, width)], quarter, opposite, cost=0.1)
            joined_cross = flip(joined, 1)
            (inv,) = call(functools.partial(pivot_kernel, middle, width), [square], half)
            inv, other_half = lax.optimization_barrier((inv, other_half))
            (last_half,) = call(add_kernel, [last_half.shape], last_half, other_half, cost=0.1)
            cross = flip(last_half, 1)
            total, coef, key = call(
                functools.partial(
                    near_update, width, count, functools.partial(take_quarters, plan)
                ),
                [(plan.rows3, width), (count, width), square],
                place,
                joined,
                joined_cross,
                inv,
                smem=1,
            )
            (rest,) = call(
                functools.partial(joined_update, plan, width, count, below),
                [(following, width)],
                place,
                last_half,
                cross,
                total,
                coef,
                smem=1,
                scratch=[pltpu.VMEM((plan.last3, width), F32)],
            )
        else:
            other_key = partner(key, level, inner_bits)
            sent_rest = rest
            if level == 0:
                sent_rest, other_key = lax.optimization_barrier((rest, other_key))
            other_rest = partner(sent_rest, level, inner_bits)
            (inv,) = call(functools.partial(pivot_kernel, 0, width), [square], key, other_key)
            total, coef, key = call(
                functools.partial(near_update, width, count, take_full),
                [(counts[level], width), (count, width), square],
                rest,
                other_rest,
                inv,
            )
            if spread and level == 0:
                parts = []
                for first, size, sent in (
                    (0, plan.near, plan.near2),
                    (plan.near, plan.far, plan.near3 + plan.far3),
                ):
                    parts += call(
                        functools.partial(part_update, plan, width, count, below, first),
                        [(size, width), (sent, width)],
                        place,
                        rest,
                        other_rest,
                        total,
                        coef,
                        cost=0.4,
                        smem=1,
                    )
                    total, _ = lax.optimization_barrier((total, parts[-1]))
                rest_near, mine, rest_far, send = parts
            else:
                (rest,) = call(
                    functools.partial(far_update, width, count, below),
                    [(following, width)],
                    rest,
                    other_rest,
                    total,
                    coef,
                )
        coefs.append(coef)
    last = jnp.concatenate([key, rest], axis=0)
    other_last = partner(last, levels - 1, inner_bits)
    (folded,) = call(
        functools.partial(fold_kernel, levels, width, nrhs),
        [(width + nrhs, leaf_rows)],
        weights,
        *coefs,
    )
    (result,) = call(
        functools.partial(final_kernel, width), [(nrhs, leaf_rows)], last, other_last, folded
    )
    return result.T


def solution(mesh):
    placed = (
        P(("rowa", "rowb"), None),
        P(("rowa", "rowb"), None),
        P(None, ("rowa", "rowb"), None),
        P(),
    )
    return jax.shard_map(
        body, mesh=mesh, in_specs=placed, out_specs=P(("rowa", "rowb"), None), check_vma=False
    )
```

```python
import functools

import jax
import jax.numpy as jnp
from jax import lax
from jax.experimental import pallas as pl
from jax.experimental.pallas import tpu as pltpu
from jax.sharding import PartitionSpec as P

F32 = jnp.float32
BF16 = jnp.bfloat16
STEP = 16
VMEM_LIMIT = 48 * 1024 * 1024
LEAF_LIMIT = 48 * 1024 * 1024


def split3(value):
    high = value.astype(BF16)
    rest = value - high.astype(F32)
    middle = rest.astype(BF16)
    return high, middle, (rest - middle.astype(F32)).astype(BF16)


def left6(value):
    high, middle, low = split3(value)
    return jnp.concatenate([high, high, middle, high, middle, low], axis=1)


def right6(value, axis):
    high, middle, low = split3(value)
    return jnp.concatenate([high, middle, high, low, middle, high], axis=axis)


def pad_rows(value):
    extra = -value.shape[0] % 16
    if not extra:
        return value
    return jnp.concatenate([value, jnp.zeros((extra, value.shape[1]), value.dtype)], axis=0)


def dot(left, right):
    product = jnp.dot(left6(pad_rows(left)), right6(right, 0), preferred_element_type=F32)
    return product[: left.shape[0]]


def dot_nt(left, right):
    product = dot6_nt(left6(pad_rows(left)), right6(right, 1))
    return product[: left.shape[0]]


def dot6_nt(left, right):
    return lax.dot_general(left, right, (((1,), (1,)), ((), ())), preferred_element_type=F32)


def spread_row(value, index):
    return jnp.broadcast_to(value[index : index + 1, :], value.shape)


def eliminate(panel, pivots):
    sub = lax.broadcasted_iota(jnp.int32, panel[0].shape, 0)
    pieces = range(len(panel))
    pivot = spread_row(pivots[0][0], 0)
    for step in range(STEP):
        piece, index = divmod(step, 8)
        scale = pltpu.reciprocal(pivot, approx=True)
        if step + 1 < STEP:
            next_piece, next_index = divmod(step + 1, 8)
            cross = spread_row(pivots[step][next_piece], next_index) * spread_row(
                pivots[step + 1][piece], index
            )
            pivot = spread_row(pivots[step + 1][next_piece], next_index) - cross * scale
        own = sub == index
        factors = [
            (jnp.where(own, -1.0, pivots[step][at]) if at == piece else pivots[step][at]) * scale
            for at in pieces
        ]

        def reduce(column):
            row = spread_row(column[piece], index)
            return [
                (jnp.where(own, 0.0, column[at]) if at == piece else column[at]) - factors[at] * row
                for at in pieces
            ]

        panel = reduce(panel)
        for later in range(step + 1, STEP):
            pivots[later] = reduce(pivots[later])
    return panel


def sweep(matrix, first, last, tick=lambda: None):
    size = matrix.shape[0]
    pieces = range(STEP // 8)
    lane = lax.broadcasted_iota(jnp.int32, (8, size), 1)
    sub = lax.broadcasted_iota(jnp.int32, (8, size), 0)
    lane_all = lax.broadcasted_iota(jnp.int32, (size, size), 1)
    sub_all = lax.broadcasted_iota(jnp.int32, (size, size), 0)
    rows = [matrix[first + 8 * at : first + 8 * at + 8] for at in pieces]
    for start in range(first, last, STEP):
        stop = start + STEP
        more = stop < size
        pivots = [
            [jnp.broadcast_to(rows[at][:, start + index : start + index + 1], (8, size)) for at in pieces]
            for index in range(STEP)
        ]
        inside = (lane >= start) & (lane < stop)
        panel = [
            jnp.where(inside, jnp.where(lane - start == sub + 8 * at, 1.0, 0.0), rows[at])
            for at in pieces
        ]
        row_inside = (sub_all >= start) & (sub_all < stop)
        lane_inside = (lane_all >= start) & (lane_all < stop)
        column = jnp.where(row_inside, 0.0, matrix)[:, start:stop]
        base = jnp.where(row_inside | lane_inside, 0.0, matrix)
        following = []
        if more:
            following = [matrix[stop + 8 * at : stop + 8 * at + 8] for at in pieces]
        ahead = [
            [jnp.broadcast_to(piece[:, start + index : start + index + 1], (8, size)) for piece in following]
            for index in range(STEP)
        ]
        tick()
        panel = eliminate(panel, pivots)
        if more:
            rows = []
            for at in pieces:
                terms = [
                    ahead[index][at] * spread_row(panel[index // 8], index % 8)
                    for index in range(STEP)
                ]
                while len(terms) > 1:
                    terms = [terms[at2] + terms[at2 + 1] for at2 in range(0, len(terms), 2)]
                rows.append(base[stop + 8 * at : stop + 8 * at + 8] - terms[0])
        joined = jnp.concatenate(panel, axis=0)
        matrix = base - jnp.dot(left6(column), right6(joined, 0), preferred_element_type=F32)
        parts = [matrix[:start]] if start else []
        parts.append(joined)
        if more:
            parts += rows
        if stop + (STEP if more else 0) < size:
            parts.append(matrix[stop + STEP :])
        matrix = jnp.concatenate(parts, axis=0)
    return matrix


def inverse(matrix, tick=lambda: None):
    return sweep(matrix, 0, matrix.shape[0], tick)


def add_eye(matrix):
    row = lax.broadcasted_iota(jnp.int32, matrix.shape, 0)
    column = lax.broadcasted_iota(jnp.int32, matrix.shape, 1)
    return matrix + jnp.where(row == column, 1.0, 0.0)


def gram_pair(levels, width, count, level, v6_ref, s6_ref):
    low = level * width
    pair = min(2, levels - level)
    product = dot6_nt(v6_ref[low:, :], s6_ref[low : low + pair * width, :])
    result = []
    for index in range(pair):
        value = product[index * width : count - low, index * width : (index + 1) * width]
        offset = sum(count - done * width for done in range(level + index)) - width
        if offset < 0:
            result.append((offset, value[:width]))
            value = value[width:]
            offset = 0
        result.append((offset, value))
    return result


def leaf_kernel(levels, width, blocks, place_ref, ranks_hbm, rhs_hbm, leaf_hbm, bases_hbm, *refs):
    key_ref, rest_ref, scaled_ref, lower_ref, v6_ref, s6_ref, v_ref, *refs = refs
    ranks_ref, rhs_ref, leaf_ref, bases_ref, sem = refs
    nrhs = rhs_ref.shape[0]
    place = place_ref[0]
    rows = levels * width
    count = rows + nrhs
    padded = v6_ref.shape[0]
    spans = [slice(block * width, (block + 1) * width) for block in range(blocks)]
    leaf_copies = [
        pltpu.make_async_copy(leaf_hbm.at[span], leaf_ref.at[span], sem.at[index])
        for index, span in enumerate(spans)
    ]
    other_copies = [
        pltpu.make_async_copy(bases_hbm, bases_ref, sem.at[blocks]),
        pltpu.make_async_copy(rhs_hbm, rhs_ref, sem.at[blocks + 1]),
        pltpu.make_async_copy(ranks_hbm, ranks_ref, sem.at[blocks + 2]),
    ]
    for copy in leaf_copies + other_copies:
        copy.start()

    tasks = []
    quota = [0]

    def tick():
        for _ in range(min(quota[0], len(tasks))):
            tasks.pop(0)()

    def run(steps):
        quota[0] = -(-len(tasks) // steps)

    def arrive():
        for copy in leaf_copies[1:] + other_copies:
            copy.wait()

    def load(block, level):
        sub = lax.broadcasted_iota(jnp.int32, (width, width), 0)
        rank = ranks_ref[2 ** (levels - level) + lax.shift_right_logical(place, level) - 1]
        piece = jnp.where(sub < rank, bases_ref[level - 1, spans[block], :].T, 0.0)
        span = slice((level - 1) * width, level * width)
        v_ref[block, span, :] = piece
        if block == 0:
            v6_ref[span, :] = left6(piece)

    def load_rhs():
        for block, span in enumerate(spans):
            piece = rhs_ref[:, span]
            piece = jnp.concatenate([piece, jnp.zeros((padded - count, width), F32)], axis=0)
            v_ref[block, rows:padded, :] = piece
            if block == 0:
                v6_ref[rows:padded, :] = left6(piece)

    chunk = up(padded // 3, 16)
    chunks = [slice(at, min(at + chunk, padded)) for at in range(0, padded, chunk)]

    def split_values(block, span):
        v6_ref[span, :] = left6(v_ref[block, span, :])

    def apply(block, weights, span):
        product = jnp.dot(v6_ref[span, :], weights, preferred_element_type=F32)
        scaled = product[:, :width]
        scaled_ref[block, span, :] = scaled
        stop = min(span.stop, rows)
        if span.start < stop:
            s6_ref[span.start : stop, :] = right6(scaled[: stop - span.start], 1)
        for later in range(block + 1, blocks):
            at = (later - block) * width
            v_ref[later, span, :] = v_ref[later, span, :] - product[:, at : at + width]

    def gram(block, level):
        for offset, value in gram_pair(levels, width, count, level, v6_ref, s6_ref):
            target = key_ref if offset < 0 else rest_ref
            span = slice(max(offset, 0), max(offset, 0) + value.shape[0])
            target[span, :] = value if block == 0 else target[span, :] + value

    leaf_copies[0].wait()
    tasks.append(arrive)
    tasks += [functools.partial(load, 0, level) for level in range(1, levels + 1)]
    tasks.append(load_rhs)
    for block in range(1, blocks):
        tasks += [functools.partial(load, block, level) for level in range(1, levels + 1)]
    schur = {(0, 0): leaf_ref[spans[0], spans[0]]}
    for block in range(blocks):
        run(width // STEP)
        inv = inverse(schur[block, block], tick)
        while tasks:
            tasks.pop(0)()
        if block == 0:
            for first in range(blocks):
                for second in range(blocks):
                    if first or second:
                        schur[first, second] = leaf_ref[spans[first], spans[second]]
        rest = range(block + 1, blocks)
        weights = right6(inv, 0)
        if rest:
            right = jnp.concatenate([schur[block, later] for later in rest], axis=1)
            upper = dot(inv, right)
            split = right6(upper, 0)
            for index, later in enumerate(rest):
                lower_ref[block, later - 1] = upper[:, index * width : (index + 1) * width]

            def reduce(first, block=block, rest=rest, split=split):
                product = jnp.dot(left6(schur[first, block]), split, preferred_element_type=F32)
                for index, later in enumerate(rest):
                    at = slice(index * width, (index + 1) * width)
                    schur[first, later] = schur[first, later] - product[:, at]

            reduce(block + 1)
            tasks += [functools.partial(reduce, first) for first in rest[1:]]
            weights = jnp.concatenate([weights, split], axis=1)
        if block:
            tasks += [functools.partial(split_values, block, span) for span in chunks]
        tasks += [functools.partial(apply, block, weights, span) for span in chunks]
        if block < blocks - 1:
            tasks += [functools.partial(gram, block, level) for level in range(0, levels, 2)]
    while tasks:
        tasks.pop(0)()
    key = dot6_nt(v6_ref[:width, :], s6_ref[:width, :])
    key_ref[...] = key_ref[...] + key if blocks > 1 else key
    if blocks == 1:
        rest_ref[...] = jnp.zeros_like(rest_ref)


def gram_kernel(levels, width, count, part_ref, v6_ref, s6_ref, rest_ref):
    for level in range(0, levels, 2):
        for offset, value in gram_pair(levels, width, count, level, v6_ref, s6_ref):
            if offset >= 0:
                span = slice(offset, offset + value.shape[0])
                rest_ref[span, :] = part_ref[span, :] + value


def pivot_kernel(first, last, *refs):
    if first == 0:
        matrix = add_eye(refs[0][...] + refs[1][...])
    else:
        matrix = refs[0][...]
    refs[-1][...] = sweep(matrix, first, last)


def near_update(width, count, take, *refs):
    rest_ref, coef_ref, key_ref = refs[-3:]
    inv_ref = refs[-4]
    take(refs[:-4], rest_ref)
    coef_ref[...] = dot(rest_ref[:count], inv_ref[...])
    next_key(width, count, rest_ref, coef_ref, key_ref)


def last_update(width, count, own_ref, other_ref, inv_ref, coef_ref, last_ref):
    rest = own_ref[:count] + other_ref[:count]
    coef_ref[...] = dot(rest, inv_ref[...])
    total = own_ref[count:] + other_ref[count:]
    last_ref[...] = total - dot_nt(coef_ref[...], rest[:width])


def next_key(width, count, rest_ref, coef_ref, key_ref):
    key_ref[...] = rest_ref[count : count + width] - dot_nt(coef_ref[:width], rest_ref[:width])


def take_full(refs, rest_ref):
    own_ref, other_ref = refs
    rows = rest_ref.shape[0]
    rest_ref[...] = own_ref[:rows] + other_ref[:rows]


def take_halves(plan, refs, rest_ref):
    place_ref, own_ref, near_ref, cross_ref = refs
    side = place_ref[0] & 1
    for index, source in ((side, near_ref), (side ^ 1, cross_ref)):
        span = pl.ds(plan.near2_at(index), plan.near2)
        rest_ref[span, :] = own_ref[span, :] + source[...]


def take_quarters(plan, refs, rest_ref):
    place_ref, joined_ref, cross_ref = refs
    for index in range(4):
        source, at = (joined_ref, cross_ref)[index & 1], (index // 2) * plan.near3
        span = pl.ds(plan.near3_at((place_ref[0] & 3) ^ index), plan.near3)
        rest_ref[span, :] = source[at : at + plan.near3, :]


def rank_update(width, count, below, first, last, rest_ref, coef_ref, put):
    offset = 0
    for level in range(below):
        low = level * width
        start = low + width if level == 0 else low
        size = count - start
        begin, end = max(first - offset, 0), min(last - offset, size)
        if begin < end:
            product = dot_nt(coef_ref[start + begin : start + end, :], rest_ref[low : low + width, :])
            put(offset + begin, product)
        offset += size


def far_update(width, count, below, own_ref, other_ref, rest_ref, coef_ref, out_ref):
    skip = count + width

    def put(offset, product):
        span = slice(skip + offset, skip + offset + product.shape[0])
        out_ref[offset : offset + product.shape[0], :] = own_ref[span, :] + other_ref[span, :] - product

    rank_update(width, count, below, 0, out_ref.shape[0], rest_ref, coef_ref, put)


def part_update(plan, width, count, below, first, place_ref, *refs):
    own_ref, other_ref, rest_ref, coef_ref, out_ref, *send_refs = refs
    skip = count + width
    place = place_ref[0]

    def put(offset, product):
        span = slice(skip + offset, skip + offset + product.shape[0])
        at = offset - first
        out_ref[at : at + product.shape[0], :] = own_ref[span, :] + other_ref[span, :] - product

    rank_update(width, count, below, first, first + out_ref.shape[0], rest_ref, coef_ref, put)
    if first == 0:
        send_refs[0][...] = out_ref[pl.ds(plan.near2_at(place & 1), plan.near2), :]
    else:
        send_refs[0][...] = out_ref[pl.ds(plan.near3_at((place & 3) ^ 2), plan.near3), :]
        send_refs[1][...] = out_ref[pl.ds(plan.rows3 + plan.far3_at(place & 1), plan.far3), :]


def quarter_update(plan, width, count, below, *refs):
    place_ref, own_ref, near_ref, cross_ref, far_own_ref, far_ref, inv_ref = refs[:7]
    rest_ref, coef_ref, out_ref, product_ref = refs[7:]
    take_halves(plan, (place_ref, own_ref, near_ref, cross_ref), rest_ref)
    coef_ref[...] = dot(rest_ref[:count], inv_ref[...])

    def put(offset, product):
        product_ref[offset : offset + product.shape[0], :] = product

    rank_update(width, count, below, 0, plan.rows3, rest_ref, coef_ref, put)
    span = pl.ds(plan.near3_at(place_ref[0] & 3), plan.near3)
    out_ref[...] = far_own_ref[span, :] + far_ref[...] - product_ref[span, :]


def half_update(plan, width, count, below, *refs):
    place_ref, rest_ref, coef_ref, own_ref, far_ref, out_ref, product_ref = refs

    def put(offset, product):
        at = offset - plan.rows3
        product_ref[at : at + product.shape[0], :] = product

    rank_update(width, count, below, plan.rows3, plan.far, rest_ref, coef_ref, put)
    at = plan.far3_at(place_ref[0] & 1)
    out_ref[...] = (
        own_ref[pl.ds(plan.rows3 + at, plan.far3), :]
        + far_ref[...]
        - product_ref[pl.ds(at, plan.far3), :]
    )


def joined_update(plan, width, count, below, *refs):
    place_ref, half_ref, cross_ref, rest_ref, coef_ref, out_ref, total_ref = refs
    side = place_ref[0] & 1
    for index, source in ((side, half_ref), (side ^ 1, cross_ref)):
        total_ref[pl.ds(plan.far3_at(index), plan.far3), :] = source[...]

    def put(offset, product):
        span = slice(offset, offset + product.shape[0])
        out_ref[span, :] = total_ref[span, :] - product

    rank_update(width, count, below, 0, out_ref.shape[0], rest_ref, coef_ref, put)


def add_kernel(own_ref, other_ref, out_ref):
    out_ref[...] = own_ref[...] + other_ref[...]


def join_kernel(first_ref, second_ref, out_ref):
    rows = first_ref.shape[0]
    out_ref[:rows] = first_ref[...]
    out_ref[rows:] = second_ref[...]


def back_kernel(width, blocks, scaled_ref, lower_ref, out_ref):
    values = [None] * blocks
    for block in reversed(range(blocks)):
        value = scaled_ref[block]
        for later in range(block + 1, blocks):
            value = value - dot_nt(values[later], lower_ref[block, later - 1])
        values[block] = value
        out_ref[:, block * width : (block + 1) * width] = value


def fold_kernel(levels, width, nrhs, weights_ref, *refs):
    coef_refs, out_ref = refs[:-1], refs[-1]
    known = [None] * (levels - 1)
    for level in reversed(range(levels - 1)):
        coef = coef_refs[level]
        value = coef[(levels - 2 - level) * width :, :]
        above = range(level + 1, levels - 1)
        if above:
            value = value - dot(
                jnp.concatenate([known[later] for later in above], axis=1),
                coef[: len(above) * width, :],
            )
        known[level] = value
    low = (levels - 1) * width
    out_ref[...] = weights_ref[low : low + width + nrhs, :] - dot(
        jnp.concatenate(known, axis=1), weights_ref[:low, :]
    )


def final_kernel(width, own_ref, other_ref, folded_ref, out_ref):
    inv = inverse(add_eye(own_ref[:width] + other_ref[:width]))
    coef = dot(own_ref[width:] + other_ref[width:], inv)
    out_ref[...] = folded_ref[width:, :] - dot(coef, folded_ref[:width, :])


def call(kernel, shapes, *operands, cost=1.5, smem=0, hbm=0, scratch=(), limit=VMEM_LIMIT):
    flops = int(cost * 10**9)
    space = [pl.BlockSpec(memory_space=pltpu.SMEM)] * smem
    space += [pl.BlockSpec(memory_space=pltpu.VMEM)] * (len(operands) - smem - hbm)
    space += [pl.BlockSpec(memory_space=pltpu.HBM)] * hbm
    outs = [
        shape if isinstance(shape, jax.ShapeDtypeStruct) else jax.ShapeDtypeStruct(shape, F32)
        for shape in shapes
    ]
    return pl.pallas_call(
        kernel,
        out_shape=outs,
        in_specs=space,
        out_specs=[pl.BlockSpec(memory_space=pltpu.VMEM)] * len(outs),
        scratch_shapes=list(scratch),
        compiler_params=pltpu.CompilerParams(vmem_limit_bytes=limit),
        cost_estimate=pl.CostEstimate(flops=flops, bytes_accessed=flops // 300, transcendentals=0),
    )(*operands)


def flip(value, mask, axis="rowb"):
    pairs = [(source, source ^ mask) for source in range(lax.axis_size(axis))]
    return lax.ppermute(value, axis, pairs)


def partner(value, level, inner_bits):
    if level < inner_bits:
        return flip(value, 2**level)
    return flip(value, 2 ** (level - inner_bits), "rowa")


def up(value, step):
    return -(-value // step) * step


class Plan:
    def __init__(self, near, rows3, last3):
        self.near, self.rows3, self.last3, self.far = near, rows3, last3, rows3 + last3
        self.near2 = up(near, 16) // 2
        self.near3 = up(rows3, 32) // 4
        self.far3 = up(last3, 16) // 2

    def near2_at(self, side):
        return pl.multiple_of(side * (self.near - self.near2), 8)

    def near3_at(self, index):
        return pl.multiple_of(jnp.minimum(index * self.near3, self.rows3 - self.near3), 8)

    def far3_at(self, side):
        return pl.multiple_of(side * (self.last3 - self.far3), 8)


def body(right_side, leaves, bases, ranks):
    levels = bases.shape[0]
    leaf_rows = leaves.shape[0]
    width = bases.shape[2]
    nrhs = right_side.shape[1]
    blocks = leaf_rows // width
    inner_bits = lax.axis_size("rowb").bit_length() - 1
    place = lax.axis_index("rowa") * lax.axis_size("rowb") + lax.axis_index("rowb")
    place = place.astype(jnp.int32).reshape(1)
    rows = levels * width + nrhs
    padded = up(rows, 16)
    counts = [rows - level * width for level in range(levels)]
    spread = inner_bits >= 3 and levels >= 4
    plan = None
    if spread:
        plan = Plan(counts[1], counts[2], sum(counts[3:]) - width)
    square = (width, width)
    middle = up(width // 2, STEP)
    key, part, scaled, lower, values6, scaled6 = call(
        functools.partial(leaf_kernel, levels, width, blocks),
        [
            square,
            (sum(counts) - width, width),
            (blocks, padded, width),
            (blocks, max(blocks - 1, 1)) + square,
            jax.ShapeDtypeStruct((padded, 6 * width), BF16),
            jax.ShapeDtypeStruct((levels * width, 6 * width), BF16),
        ],
        place,
        *[
            pltpu.with_memory_space_constraint(each, pltpu.HBM)
            for each in (ranks, right_side.T, leaves, bases)
        ],
        smem=1,
        hbm=4,
        limit=LEAF_LIMIT,
        scratch=[
            pltpu.VMEM((blocks, padded, width), F32),
            pltpu.SMEM(ranks.shape, jnp.int32),
            pltpu.VMEM((nrhs, leaf_rows), F32),
            pltpu.VMEM((leaf_rows, leaf_rows), F32),
            pltpu.VMEM((levels, leaf_rows, width), F32),
            pltpu.SemaphoreType.DMA((blocks + 3,)),
        ],
    )
    (rest,) = call(
        functools.partial(gram_kernel, levels, width, rows),
        [(sum(counts) - width, width)],
        part,
        values6,
        scaled6,
    )
    if not spread:
        (weights,) = call(
            functools.partial(back_kernel, width, blocks), [(padded, leaf_rows)], scaled, lower
        )
    coefs = []
    for level in range(levels - 1):
        count = counts[level] - width
        below = levels - 1 - level
        following = sum(counts[level + 1 :]) - width
        if spread and level == 1:
            other_key = partner(key, level, inner_bits)
            near = partner(mine, level, inner_bits)
            far = partner(send, level, inner_bits)
            (half,) = call(functools.partial(pivot_kernel, 0, middle), [square], key, other_key)
            send_last, half = lax.optimization_barrier((send_last, half))
            far_last = partner(send_last, level, inner_bits)
            half, near = lax.optimization_barrier((half, near))
            cross = flip(near, 1)
            (inv,) = call(functools.partial(pivot_kernel, middle, width), [square], half)
            total, coef, quarter = call(
                functools.partial(quarter_update, plan, width, count, below),
                [(plan.near, width), (count, width), (plan.near3, width)],
                place,
                rest_near,
                near,
                cross,
                rest_far,
                far,
                inv,
                smem=1,
                scratch=[pltpu.VMEM((plan.rows3, width), F32)],
            )
            (key,) = call(functools.partial(next_key, width, count), [square], total, coef, cost=0.3)
        elif spread and level == 2:
            other_quarter = partner(quarter, level, inner_bits)
            other_key = partner(key, level, inner_bits)
            scaled, key = lax.optimization_barrier((scaled, key))
            (weights,) = call(
                functools.partial(back_kernel, width, blocks),
                [(padded, leaf_rows)],
                scaled,
                lower,
                cost=1.0,
            )
            quarter, weights = lax.optimization_barrier((quarter, weights))
            (quarter,) = call(add_kernel, [quarter.shape], quarter, other_quarter, cost=0.1)
            opposite = flip(quarter, 2)
            far_last, _ = lax.optimization_barrier((far_last, quarter))
            (last_half,) = call(
                functools.partial(half_update, plan, width, counts[1] - width, levels - 2),
                [(plan.far3, width)],
                place,
                total,
                coefs[1],
                rest_far,
                far_last,
                cost=0.3,
                smem=1,
                scratch=[pltpu.VMEM((plan.last3, width), F32)],
            )
            other_half = partner(last_half, level, inner_bits)
            other_key, _ = lax.optimization_barrier((other_key, last_half))
            (half,) = call(functools.partial(pivot_kernel, 0, middle), [square], key, other_key)
            half, opposite = lax.optimization_barrier((half, opposite))
            (joined,) = call(join_kernel, [(2 * plan.near3, width)], quarter, opposite, cost=0.1)
            joined_cross = flip(joined, 1)
            (inv,) = call(functools.partial(pivot_kernel, middle, width), [square], half)
            inv, other_half = lax.optimization_barrier((inv, other_half))
            (last_half,) = call(add_kernel, [last_half.shape], last_half, other_half, cost=0.1)
            cross = flip(last_half, 1)
            total, coef, key = call(
                functools.partial(
                    near_update, width, count, functools.partial(take_quarters, plan)
                ),
                [(plan.rows3, width), (count, width), square],
                place,
                joined,
                joined_cross,
                inv,
                smem=1,
            )
            (rest,) = call(
                functools.partial(joined_update, plan, width, count, below),
                [(following, width)],
                place,
                last_half,
                cross,
                total,
                coef,
                smem=1,
                scratch=[pltpu.VMEM((plan.last3, width), F32)],
            )
        else:
            other_key = partner(key, level, inner_bits)
            sent_rest = rest
            if level == 0:
                sent_rest, other_key = lax.optimization_barrier((rest, other_key))
            other_rest = partner(sent_rest, level, inner_bits)
            (inv,) = call(functools.partial(pivot_kernel, 0, width), [square], key, other_key)
            if level == levels - 2:
                coef, last = call(
                    functools.partial(last_update, width, count),
                    [(count, width), (counts[level + 1], width)],
                    rest,
                    other_rest,
                    inv,
                )
                coefs.append(coef)
                continue
            total, coef, key = call(
                functools.partial(near_update, width, count, take_full),
                [(counts[level], width), (count, width), square],
                rest,
                other_rest,
                inv,
            )
            if spread and level == 0:
                parts = []
                for first, size, sent in (
                    (0, plan.near, [plan.near2]),
                    (plan.near, plan.far, [plan.near3, plan.far3]),
                ):
                    parts += call(
                        functools.partial(part_update, plan, width, count, below, first),
                        [(each, width) for each in [size] + sent],
                        place,
                        rest,
                        other_rest,
                        total,
                        coef,
                        cost=0.4,
                        smem=1,
                    )
                    total, _ = lax.optimization_barrier((total, parts[-1]))
                rest_near, mine, rest_far, send, send_last = parts
            else:
                (rest,) = call(
                    functools.partial(far_update, width, count, below),
                    [(following, width)],
                    rest,
                    other_rest,
                    total,
                    coef,
                )
        coefs.append(coef)
    other_last = partner(last, levels - 1, inner_bits)
    (folded,) = call(
        functools.partial(fold_kernel, levels, width, nrhs),
        [(width + nrhs, leaf_rows)],
        weights,
        *coefs,
    )
    (result,) = call(
        functools.partial(final_kernel, width), [(nrhs, leaf_rows)], last, other_last, folded
    )
    return result.T


def solution(mesh):
    placed = (
        P(("rowa", "rowb"), None),
        P(("rowa", "rowb"), None),
        P(None, ("rowa", "rowb"), None),
        P(),
    )
    return jax.shard_map(
        body, mesh=mesh, in_specs=placed, out_specs=P(("rowa", "rowb"), None), check_vma=False
    )
```

```python
import functools

import jax
import jax.numpy as jnp
from jax import lax
from jax.experimental import pallas as pl
from jax.experimental.pallas import tpu as pltpu
from jax.sharding import PartitionSpec as P

F32 = jnp.float32
BF16 = jnp.bfloat16
STEP = 16
VMEM_LIMIT = 48 * 1024 * 1024
LEAF_LIMIT = 48 * 1024 * 1024


def split3(value):
    high = value.astype(BF16)
    rest = value - high.astype(F32)
    middle = rest.astype(BF16)
    return high, middle, (rest - middle.astype(F32)).astype(BF16)


def left6(value):
    high, middle, low = split3(value)
    return jnp.concatenate([high, high, middle, high, middle, low], axis=1)


def right6(value, axis):
    high, middle, low = split3(value)
    return jnp.concatenate([high, middle, high, low, middle, high], axis=axis)


def pad_rows(value):
    extra = -value.shape[0] % 16
    if not extra:
        return value
    return jnp.concatenate([value, jnp.zeros((extra, value.shape[1]), value.dtype)], axis=0)


def dot(left, right):
    product = jnp.dot(left6(pad_rows(left)), right6(right, 0), preferred_element_type=F32)
    return product[: left.shape[0]]


def dot_nt(left, right):
    product = dot6_nt(left6(pad_rows(left)), right6(right, 1))
    return product[: left.shape[0]]


def dot6_nt(left, right):
    return lax.dot_general(left, right, (((1,), (1,)), ((), ())), preferred_element_type=F32)


def spread_row(value, index):
    return jnp.broadcast_to(value[index : index + 1, :], value.shape)


def eliminate(panel, pivots):
    sub = lax.broadcasted_iota(jnp.int32, panel[0].shape, 0)
    pieces = range(len(panel))
    pivot = spread_row(pivots[0][0], 0)
    for step in range(STEP):
        piece, index = divmod(step, 8)
        scale = pltpu.reciprocal(pivot, approx=True)
        if step + 1 < STEP:
            next_piece, next_index = divmod(step + 1, 8)
            cross = spread_row(pivots[step][next_piece], next_index) * spread_row(
                pivots[step + 1][piece], index
            )
            pivot = spread_row(pivots[step + 1][next_piece], next_index) - cross * scale
        own = sub == index
        factors = [
            (jnp.where(own, -1.0, pivots[step][at]) if at == piece else pivots[step][at]) * scale
            for at in pieces
        ]

        def reduce(column):
            row = spread_row(column[piece], index)
            return [
                (jnp.where(own, 0.0, column[at]) if at == piece else column[at]) - factors[at] * row
                for at in pieces
            ]

        panel = reduce(panel)
        for later in range(step + 1, STEP):
            pivots[later] = reduce(pivots[later])
    return panel


def sweep(matrix, first, last, tick=lambda: None):
    size = matrix.shape[0]
    pieces = range(STEP // 8)
    lane = lax.broadcasted_iota(jnp.int32, (8, size), 1)
    sub = lax.broadcasted_iota(jnp.int32, (8, size), 0)
    lane_all = lax.broadcasted_iota(jnp.int32, (size, size), 1)
    sub_all = lax.broadcasted_iota(jnp.int32, (size, size), 0)
    rows = [matrix[first + 8 * at : first + 8 * at + 8] for at in pieces]
    for start in range(first, last, STEP):
        stop = start + STEP
        more = stop < size
        pivots = [
            [jnp.broadcast_to(rows[at][:, start + index : start + index + 1], (8, size)) for at in pieces]
            for index in range(STEP)
        ]
        inside = (lane >= start) & (lane < stop)
        panel = [
            jnp.where(inside, jnp.where(lane - start == sub + 8 * at, 1.0, 0.0), rows[at])
            for at in pieces
        ]
        row_inside = (sub_all >= start) & (sub_all < stop)
        lane_inside = (lane_all >= start) & (lane_all < stop)
        column = jnp.where(row_inside, 0.0, matrix)[:, start:stop]
        base = jnp.where(row_inside | lane_inside, 0.0, matrix)
        following = []
        if more:
            following = [matrix[stop + 8 * at : stop + 8 * at + 8] for at in pieces]
        ahead = [
            [jnp.broadcast_to(piece[:, start + index : start + index + 1], (8, size)) for piece in following]
            for index in range(STEP)
        ]
        tick()
        panel = eliminate(panel, pivots)
        if more:
            rows = []
            for at in pieces:
                terms = [
                    ahead[index][at] * spread_row(panel[index // 8], index % 8)
                    for index in range(STEP)
                ]
                while len(terms) > 1:
                    terms = [terms[at2] + terms[at2 + 1] for at2 in range(0, len(terms), 2)]
                rows.append(base[stop + 8 * at : stop + 8 * at + 8] - terms[0])
        joined = jnp.concatenate(panel, axis=0)
        matrix = base - jnp.dot(left6(column), right6(joined, 0), preferred_element_type=F32)
        parts = [matrix[:start]] if start else []
        parts.append(joined)
        if more:
            parts += rows
        if stop + (STEP if more else 0) < size:
            parts.append(matrix[stop + STEP :])
        matrix = jnp.concatenate(parts, axis=0)
    return matrix


def inverse(matrix, tick=lambda: None):
    return sweep(matrix, 0, matrix.shape[0], tick)


def add_eye(matrix):
    row = lax.broadcasted_iota(jnp.int32, matrix.shape, 0)
    column = lax.broadcasted_iota(jnp.int32, matrix.shape, 1)
    return matrix + jnp.where(row == column, 1.0, 0.0)


def gram_pair(levels, width, count, level, v6_ref, s6_ref):
    low = level * width
    pair = min(2, levels - level)
    product = dot6_nt(v6_ref[low:, :], s6_ref[low : low + pair * width, :])
    result = []
    for index in range(pair):
        value = product[index * width : count - low, index * width : (index + 1) * width]
        offset = sum(count - done * width for done in range(level + index)) - width
        if offset < 0:
            result.append((offset, value[:width]))
            value = value[width:]
            offset = 0
        result.append((offset, value))
    return result


def leaf_kernel(levels, width, blocks, place_ref, ranks_hbm, rhs_hbm, leaf_hbm, bases_hbm, *refs):
    key_ref, rest_ref, scaled_ref, lower_ref, v6_ref, s6_ref, v_ref, *refs = refs
    ranks_ref, rhs_ref, leaf_ref, bases_ref, sem = refs
    nrhs = rhs_ref.shape[0]
    place = place_ref[0]
    rows = levels * width
    count = rows + nrhs
    padded = v6_ref.shape[0]
    spans = [slice(block * width, (block + 1) * width) for block in range(blocks)]
    leaf_copies = [
        pltpu.make_async_copy(leaf_hbm.at[span], leaf_ref.at[span], sem.at[index])
        for index, span in enumerate(spans)
    ]
    other_copies = [
        pltpu.make_async_copy(bases_hbm, bases_ref, sem.at[blocks]),
        pltpu.make_async_copy(rhs_hbm, rhs_ref, sem.at[blocks + 1]),
        pltpu.make_async_copy(ranks_hbm, ranks_ref, sem.at[blocks + 2]),
    ]
    for copy in leaf_copies + other_copies:
        copy.start()

    tasks = []
    quota = [0]

    def tick():
        for _ in range(min(quota[0], len(tasks))):
            tasks.pop(0)()

    def run(steps):
        quota[0] = -(-len(tasks) // steps)

    def arrive():
        for copy in leaf_copies[1:] + other_copies:
            copy.wait()

    def load(block, level):
        sub = lax.broadcasted_iota(jnp.int32, (width, width), 0)
        rank = ranks_ref[2 ** (levels - level) + lax.shift_right_logical(place, level) - 1]
        piece = jnp.where(sub < rank, bases_ref[level - 1, spans[block], :].T, 0.0)
        span = slice((level - 1) * width, level * width)
        v_ref[block, span, :] = piece
        if block == 0:
            v6_ref[span, :] = left6(piece)

    def load_rhs():
        for block, span in enumerate(spans):
            piece = rhs_ref[:, span]
            piece = jnp.concatenate([piece, jnp.zeros((padded - count, width), F32)], axis=0)
            v_ref[block, rows:padded, :] = piece
            if block == 0:
                v6_ref[rows:padded, :] = left6(piece)

    chunk = up(padded // 3, 16)
    chunks = [slice(at, min(at + chunk, padded)) for at in range(0, padded, chunk)]

    def split_values(block, span):
        v6_ref[span, :] = left6(v_ref[block, span, :])

    def apply(block, weights, span):
        product = jnp.dot(v6_ref[span, :], weights, preferred_element_type=F32)
        scaled = product[:, :width]
        scaled_ref[block, span, :] = scaled
        stop = min(span.stop, rows)
        if span.start < stop:
            s6_ref[span.start : stop, :] = right6(scaled[: stop - span.start], 1)
        for later in range(block + 1, blocks):
            at = (later - block) * width
            v_ref[later, span, :] = v_ref[later, span, :] - product[:, at : at + width]

    def gram(block, level):
        for offset, value in gram_pair(levels, width, count, level, v6_ref, s6_ref):
            target = key_ref if offset < 0 else rest_ref
            span = slice(max(offset, 0), max(offset, 0) + value.shape[0])
            target[span, :] = value if block == 0 else target[span, :] + value

    leaf_copies[0].wait()
    tasks.append(arrive)
    tasks += [functools.partial(load, 0, level) for level in range(1, levels + 1)]
    tasks.append(load_rhs)
    for block in range(1, blocks):
        tasks += [functools.partial(load, block, level) for level in range(1, levels + 1)]
    schur = {(0, 0): leaf_ref[spans[0], spans[0]]}
    for block in range(blocks):
        run(width // STEP)
        inv = inverse(schur[block, block], tick)
        while tasks:
            tasks.pop(0)()
        if block == 0:
            for first in range(blocks):
                for second in range(blocks):
                    if first or second:
                        schur[first, second] = leaf_ref[spans[first], spans[second]]
        rest = range(block + 1, blocks)
        weights = right6(inv, 0)
        if rest:
            right = jnp.concatenate([schur[block, later] for later in rest], axis=1)
            upper = dot(inv, right)
            split = right6(upper, 0)
            for index, later in enumerate(rest):
                lower_ref[block, later - 1] = upper[:, index * width : (index + 1) * width]

            def reduce(first, block=block, rest=rest, split=split):
                product = jnp.dot(left6(schur[first, block]), split, preferred_element_type=F32)
                for index, later in enumerate(rest):
                    at = slice(index * width, (index + 1) * width)
                    schur[first, later] = schur[first, later] - product[:, at]

            reduce(block + 1)
            tasks += [functools.partial(reduce, first) for first in rest[1:]]
            weights = jnp.concatenate([weights, split], axis=1)
        if block:
            tasks += [functools.partial(split_values, block, span) for span in chunks]
        tasks += [functools.partial(apply, block, weights, span) for span in chunks]
        if block < blocks - 1:
            tasks += [functools.partial(gram, block, level) for level in range(0, levels, 2)]
    while tasks:
        tasks.pop(0)()
    key = dot6_nt(v6_ref[:width, :], s6_ref[:width, :])
    key_ref[...] = key_ref[...] + key if blocks > 1 else key
    if blocks == 1:
        rest_ref[...] = jnp.zeros_like(rest_ref)


def gram_kernel(levels, width, count, part_ref, v6_ref, s6_ref, rest_ref):
    for level in range(0, levels, 2):
        for offset, value in gram_pair(levels, width, count, level, v6_ref, s6_ref):
            if offset >= 0:
                span = slice(offset, offset + value.shape[0])
                rest_ref[span, :] = part_ref[span, :] + value


def pivot_kernel(first, last, *refs):
    if first == 0:
        matrix = add_eye(refs[0][...] + refs[1][...])
    else:
        matrix = refs[0][...]
    refs[-1][...] = sweep(matrix, first, last)


def near_update(width, count, take, *refs):
    rest_ref, coef_ref, key_ref = refs[-3:]
    inv_ref = refs[-4]
    take(refs[:-4], rest_ref)
    coef_ref[...] = dot(rest_ref[:count], inv_ref[...])
    next_key(width, count, rest_ref, coef_ref, key_ref)


def last_update(width, count, own_ref, other_ref, inv_ref, coef_ref, last_ref):
    rest = own_ref[:count] + other_ref[:count]
    coef_ref[...] = dot(rest, inv_ref[...])
    total = own_ref[count:] + other_ref[count:]
    last_ref[...] = total - dot_nt(coef_ref[...], rest[:width])


def next_key(width, count, rest_ref, coef_ref, key_ref):
    key_ref[...] = rest_ref[count : count + width] - dot_nt(coef_ref[:width], rest_ref[:width])


def take_full(refs, rest_ref):
    own_ref, other_ref = refs
    rows = rest_ref.shape[0]
    rest_ref[...] = own_ref[:rows] + other_ref[:rows]


def take_halves(plan, refs, rest_ref):
    place_ref, own_ref, near_ref, cross_ref = refs
    side = place_ref[0] & 1
    for index, source in ((side, near_ref), (side ^ 1, cross_ref)):
        span = pl.ds(plan.near2_at(index), plan.near2)
        rest_ref[span, :] = own_ref[span, :] + source[...]


def take_quarters(plan, refs, rest_ref):
    place_ref, joined_ref, cross_ref = refs
    for index in range(4):
        source, at = (joined_ref, cross_ref)[index & 1], (index // 2) * plan.near3
        span = pl.ds(plan.near3_at((place_ref[0] & 3) ^ index), plan.near3)
        rest_ref[span, :] = source[at : at + plan.near3, :]


def rank_update(width, count, below, first, last, rest_ref, coef_ref, put):
    offset = 0
    for level in range(below):
        low = level * width
        start = low + width if level == 0 else low
        size = count - start
        begin, end = max(first - offset, 0), min(last - offset, size)
        if begin < end:
            product = dot_nt(coef_ref[start + begin : start + end, :], rest_ref[low : low + width, :])
            put(offset + begin, product)
        offset += size


def far_update(width, count, below, own_ref, other_ref, rest_ref, coef_ref, out_ref):
    skip = count + width

    def put(offset, product):
        span = slice(skip + offset, skip + offset + product.shape[0])
        out_ref[offset : offset + product.shape[0], :] = own_ref[span, :] + other_ref[span, :] - product

    rank_update(width, count, below, 0, out_ref.shape[0], rest_ref, coef_ref, put)


def part_update(plan, width, count, below, first, place_ref, *refs):
    own_ref, other_ref, rest_ref, coef_ref, out_ref, *send_refs = refs
    skip = count + width
    place = place_ref[0]

    def put(offset, product):
        span = slice(skip + offset, skip + offset + product.shape[0])
        at = offset - first
        out_ref[at : at + product.shape[0], :] = own_ref[span, :] + other_ref[span, :] - product

    rank_update(width, count, below, first, first + out_ref.shape[0], rest_ref, coef_ref, put)
    if first == 0:
        send_refs[0][...] = out_ref[pl.ds(plan.near2_at(place & 1), plan.near2), :]
    else:
        send_refs[0][...] = out_ref[pl.ds(plan.near3_at((place & 3) ^ 2), plan.near3), :]
        send_refs[1][...] = out_ref[pl.ds(plan.rows3 + plan.far3_at(place & 1), plan.far3), :]


def quarter_update(plan, width, count, below, *refs):
    place_ref, own_ref, near_ref, cross_ref, far_own_ref, far_ref, inv_ref = refs[:7]
    rest_ref, coef_ref, out_ref, product_ref = refs[7:]
    take_halves(plan, (place_ref, own_ref, near_ref, cross_ref), rest_ref)
    coef_ref[...] = dot(rest_ref[:count], inv_ref[...])

    def put(offset, product):
        product_ref[offset : offset + product.shape[0], :] = product

    rank_update(width, count, below, 0, plan.rows3, rest_ref, coef_ref, put)
    span = pl.ds(plan.near3_at(place_ref[0] & 3), plan.near3)
    out_ref[...] = far_own_ref[span, :] + far_ref[...] - product_ref[span, :]


def half_update(plan, width, count, below, *refs):
    place_ref, rest_ref, coef_ref, own_ref, far_ref, out_ref, product_ref = refs

    def put(offset, product):
        at = offset - plan.rows3
        product_ref[at : at + product.shape[0], :] = product

    rank_update(width, count, below, plan.rows3, plan.far, rest_ref, coef_ref, put)
    at = plan.far3_at(place_ref[0] & 1)
    out_ref[...] = (
        own_ref[pl.ds(plan.rows3 + at, plan.far3), :]
        + far_ref[...]
        - product_ref[pl.ds(at, plan.far3), :]
    )


def joined_update(plan, width, count, below, *refs):
    place_ref, half_ref, cross_ref, rest_ref, coef_ref, out_ref, total_ref = refs
    side = place_ref[0] & 1
    for index, source in ((side, half_ref), (side ^ 1, cross_ref)):
        total_ref[pl.ds(plan.far3_at(index), plan.far3), :] = source[...]

    def put(offset, product):
        span = slice(offset, offset + product.shape[0])
        out_ref[span, :] = total_ref[span, :] - product

    rank_update(width, count, below, 0, out_ref.shape[0], rest_ref, coef_ref, put)


def add_kernel(own_ref, other_ref, out_ref):
    out_ref[...] = own_ref[...] + other_ref[...]


def join_kernel(first_ref, second_ref, out_ref):
    rows = first_ref.shape[0]
    out_ref[:rows] = first_ref[...]
    out_ref[rows:] = second_ref[...]


def back_kernel(width, blocks, scaled_ref, lower_ref, out_ref):
    values = [None] * blocks
    for block in reversed(range(blocks)):
        value = scaled_ref[block]
        for later in range(block + 1, blocks):
            value = value - dot_nt(values[later], lower_ref[block, later - 1])
        values[block] = value
        out_ref[:, block * width : (block + 1) * width] = value


def fold_kernel(levels, width, nrhs, weights_ref, *refs):
    coef_refs, out_ref = refs[:-1], refs[-1]
    known = [None] * (levels - 1)
    for level in reversed(range(levels - 1)):
        coef = coef_refs[level]
        value = coef[(levels - 2 - level) * width :, :]
        above = range(level + 1, levels - 1)
        if above:
            value = value - dot(
                jnp.concatenate([known[later] for later in above], axis=1),
                coef[: len(above) * width, :],
            )
        known[level] = value
    low = (levels - 1) * width
    out_ref[...] = weights_ref[low : low + width + nrhs, :] - dot(
        jnp.concatenate(known, axis=1), weights_ref[:low, :]
    )


def final_kernel(width, own_ref, other_ref, folded_ref, out_ref):
    inv = inverse(add_eye(own_ref[:width] + other_ref[:width]))
    coef = dot(own_ref[width:] + other_ref[width:], inv)
    out_ref[...] = folded_ref[width:, :] - dot(coef, folded_ref[:width, :])


def call(kernel, shapes, *operands, cost=1.5, smem=0, hbm=0, scratch=(), limit=VMEM_LIMIT):
    flops = int(cost * 10**9)
    space = [pl.BlockSpec(memory_space=pltpu.SMEM)] * smem
    space += [pl.BlockSpec(memory_space=pltpu.VMEM)] * (len(operands) - smem - hbm)
    space += [pl.BlockSpec(memory_space=pltpu.HBM)] * hbm
    outs = [
        shape if isinstance(shape, jax.ShapeDtypeStruct) else jax.ShapeDtypeStruct(shape, F32)
        for shape in shapes
    ]
    return pl.pallas_call(
        kernel,
        out_shape=outs,
        in_specs=space,
        out_specs=[pl.BlockSpec(memory_space=pltpu.VMEM)] * len(outs),
        scratch_shapes=list(scratch),
        compiler_params=pltpu.CompilerParams(vmem_limit_bytes=limit),
        cost_estimate=pl.CostEstimate(flops=flops, bytes_accessed=flops // 300, transcendentals=0),
    )(*operands)


def flip(value, mask, axis="rowb"):
    pairs = [(source, source ^ mask) for source in range(lax.axis_size(axis))]
    return lax.ppermute(value, axis, pairs)


def partner(value, level, inner_bits):
    if level < inner_bits:
        return flip(value, 2**level)
    return flip(value, 2 ** (level - inner_bits), "rowa")


def up(value, step):
    return -(-value // step) * step


class Plan:
    def __init__(self, near, rows3, last3):
        self.near, self.rows3, self.last3, self.far = near, rows3, last3, rows3 + last3
        self.near2 = up(near, 16) // 2
        self.near3 = up(rows3, 32) // 4
        self.far3 = up(last3, 16) // 2

    def near2_at(self, side):
        return pl.multiple_of(side * (self.near - self.near2), 8)

    def near3_at(self, index):
        return pl.multiple_of(jnp.minimum(index * self.near3, self.rows3 - self.near3), 8)

    def far3_at(self, side):
        return pl.multiple_of(side * (self.last3 - self.far3), 8)


def body(right_side, leaves, bases, ranks):
    levels = bases.shape[0]
    leaf_rows = leaves.shape[0]
    width = bases.shape[2]
    nrhs = right_side.shape[1]
    blocks = leaf_rows // width
    inner_bits = lax.axis_size("rowb").bit_length() - 1
    place = lax.axis_index("rowa") * lax.axis_size("rowb") + lax.axis_index("rowb")
    place = place.astype(jnp.int32).reshape(1)
    rows = levels * width + nrhs
    padded = up(rows, 16)
    counts = [rows - level * width for level in range(levels)]
    spread = inner_bits >= 3 and levels >= 4
    plan = None
    if spread:
        plan = Plan(counts[1], counts[2], sum(counts[3:]) - width)
    square = (width, width)
    middle = up(width // 2, STEP)
    key, part, scaled, lower, values6, scaled6 = call(
        functools.partial(leaf_kernel, levels, width, blocks),
        [
            square,
            (sum(counts) - width, width),
            (blocks, padded, width),
            (blocks, max(blocks - 1, 1)) + square,
            jax.ShapeDtypeStruct((padded, 6 * width), BF16),
            jax.ShapeDtypeStruct((levels * width, 6 * width), BF16),
        ],
        place,
        *[
            pltpu.with_memory_space_constraint(each, pltpu.HBM)
            for each in (ranks, right_side.T, leaves, bases)
        ],
        smem=1,
        hbm=4,
        limit=LEAF_LIMIT,
        scratch=[
            pltpu.VMEM((blocks, padded, width), F32),
            pltpu.SMEM(ranks.shape, jnp.int32),
            pltpu.VMEM((nrhs, leaf_rows), F32),
            pltpu.VMEM((leaf_rows, leaf_rows), F32),
            pltpu.VMEM((levels, leaf_rows, width), F32),
            pltpu.SemaphoreType.DMA((blocks + 3,)),
        ],
    )
    (rest,) = call(
        functools.partial(gram_kernel, levels, width, rows),
        [(sum(counts) - width, width)],
        part,
        values6,
        scaled6,
    )
    if not spread:
        (weights,) = call(
            functools.partial(back_kernel, width, blocks), [(padded, leaf_rows)], scaled, lower
        )
    coefs = []
    for level in range(levels - 1):
        count = counts[level] - width
        below = levels - 1 - level
        following = sum(counts[level + 1 :]) - width
        if spread and level == 1:
            other_key = partner(key, level, inner_bits)
            near = partner(mine, level, inner_bits)
            far = partner(send, level, inner_bits)
            (half,) = call(functools.partial(pivot_kernel, 0, middle), [square], key, other_key)
            send_last, half = lax.optimization_barrier((send_last, half))
            far_last = partner(send_last, level, inner_bits)
            half, near = lax.optimization_barrier((half, near))
            cross = flip(near, 1)
            (inv,) = call(functools.partial(pivot_kernel, middle, width), [square], half)
            total, coef, quarter = call(
                functools.partial(quarter_update, plan, width, count, below),
                [(plan.near, width), (count, width), (plan.near3, width)],
                place,
                rest_near,
                near,
                cross,
                rest_far,
                far,
                inv,
                smem=1,
                scratch=[pltpu.VMEM((plan.rows3, width), F32)],
            )
            (key,) = call(functools.partial(next_key, width, count), [square], total, coef, cost=0.3)
        elif spread and level == 2:
            other_quarter = partner(quarter, level, inner_bits)
            other_key = partner(key, level, inner_bits)
            (last_half,) = call(
                functools.partial(half_update, plan, width, counts[1] - width, levels - 2),
                [(plan.far3, width)],
                place,
                total,
                coefs[1],
                rest_far,
                far_last,
                cost=0.3,
                smem=1,
                scratch=[pltpu.VMEM((plan.last3, width), F32)],
            )
            other_half = partner(last_half, level, inner_bits)
            other_quarter, _ = lax.optimization_barrier((other_quarter, last_half))
            (quarter,) = call(add_kernel, [quarter.shape], quarter, other_quarter, cost=0.1)
            opposite = flip(quarter, 2)
            scaled, _ = lax.optimization_barrier((scaled, quarter))
            (weights,) = call(
                functools.partial(back_kernel, width, blocks),
                [(padded, leaf_rows)],
                scaled,
                lower,
                cost=1.0,
            )
            other_key, weights = lax.optimization_barrier((other_key, weights))
            (half,) = call(functools.partial(pivot_kernel, 0, middle), [square], key, other_key)
            half, opposite = lax.optimization_barrier((half, opposite))
            (joined,) = call(join_kernel, [(2 * plan.near3, width)], quarter, opposite, cost=0.1)
            joined_cross = flip(joined, 1)
            (inv,) = call(functools.partial(pivot_kernel, middle, width), [square], half)
            inv, other_half = lax.optimization_barrier((inv, other_half))
            (last_half,) = call(add_kernel, [last_half.shape], last_half, other_half, cost=0.1)
            cross = flip(last_half, 1)
            total, coef, key = call(
                functools.partial(
                    near_update, width, count, functools.partial(take_quarters, plan)
                ),
                [(plan.rows3, width), (count, width), square],
                place,
                joined,
                joined_cross,
                inv,
                smem=1,
            )
            (rest,) = call(
                functools.partial(joined_update, plan, width, count, below),
                [(following, width)],
                place,
                last_half,
                cross,
                total,
                coef,
                smem=1,
                scratch=[pltpu.VMEM((plan.last3, width), F32)],
            )
        else:
            other_key = partner(key, level, inner_bits)
            sent_rest = rest
            if level == 0:
                sent_rest, other_key = lax.optimization_barrier((rest, other_key))
            other_rest = partner(sent_rest, level, inner_bits)
            (inv,) = call(functools.partial(pivot_kernel, 0, width), [square], key, other_key)
            if level == levels - 2:
                coef, last = call(
                    functools.partial(last_update, width, count),
                    [(count, width), (counts[level + 1], width)],
                    rest,
                    other_rest,
                    inv,
                )
                coefs.append(coef)
                continue
            total, coef, key = call(
                functools.partial(near_update, width, count, take_full),
                [(counts[level], width), (count, width), square],
                rest,
                other_rest,
                inv,
            )
            if spread and level == 0:
                parts = []
                for first, size, sent in (
                    (0, plan.near, [plan.near2]),
                    (plan.near, plan.far, [plan.near3, plan.far3]),
                ):
                    parts += call(
                        functools.partial(part_update, plan, width, count, below, first),
                        [(each, width) for each in [size] + sent],
                        place,
                        rest,
                        other_rest,
                        total,
                        coef,
                        cost=0.4,
                        smem=1,
                    )
                    total, _ = lax.optimization_barrier((total, parts[-1]))
                rest_near, mine, rest_far, send, send_last = parts
            else:
                (rest,) = call(
                    functools.partial(far_update, width, count, below),
                    [(following, width)],
                    rest,
                    other_rest,
                    total,
                    coef,
                )
        coefs.append(coef)
    other_last = partner(last, levels - 1, inner_bits)
    (folded,) = call(
        functools.partial(fold_kernel, levels, width, nrhs),
        [(width + nrhs, leaf_rows)],
        weights,
        *coefs,
    )
    (result,) = call(
        functools.partial(final_kernel, width), [(nrhs, leaf_rows)], last, other_last, folded
    )
    return result.T


def solution(mesh):
    placed = (
        P(("rowa", "rowb"), None),
        P(("rowa", "rowb"), None),
        P(None, ("rowa", "rowb"), None),
        P(),
    )
    return jax.shard_map(
        body, mesh=mesh, in_specs=placed, out_specs=P(("rowa", "rowb"), None), check_vma=False
    )
```

```python
import functools

import jax
import jax.numpy as jnp
from jax import lax
from jax.experimental import pallas as pl
from jax.experimental.pallas import tpu as pltpu
from jax.sharding import PartitionSpec as P

F32 = jnp.float32
BF16 = jnp.bfloat16
STEP = 16
VMEM_LIMIT = 48 * 1024 * 1024
LEAF_LIMIT = 48 * 1024 * 1024


def split3(value):
    high = value.astype(BF16)
    rest = value - high.astype(F32)
    middle = rest.astype(BF16)
    return high, middle, (rest - middle.astype(F32)).astype(BF16)


def left6(value):
    high, middle, low = split3(value)
    return jnp.concatenate([high, high, middle, high, middle, low], axis=1)


def right6(value, axis):
    high, middle, low = split3(value)
    return jnp.concatenate([high, middle, high, low, middle, high], axis=axis)


def pad_rows(value):
    extra = -value.shape[0] % 16
    if not extra:
        return value
    return jnp.concatenate([value, jnp.zeros((extra, value.shape[1]), value.dtype)], axis=0)


def dot(left, right):
    product = jnp.dot(left6(pad_rows(left)), right6(right, 0), preferred_element_type=F32)
    return product[: left.shape[0]]


def dot_nt(left, right):
    product = dot6_nt(left6(pad_rows(left)), right6(right, 1))
    return product[: left.shape[0]]


def dot6_nt(left, right):
    return lax.dot_general(left, right, (((1,), (1,)), ((), ())), preferred_element_type=F32)


def spread_row(value, index):
    return jnp.broadcast_to(value[index : index + 1, :], value.shape)


def eliminate(panel, pivots):
    sub = lax.broadcasted_iota(jnp.int32, panel[0].shape, 0)
    pieces = range(len(panel))
    pivot = spread_row(pivots[0][0], 0)
    for step in range(STEP):
        piece, index = divmod(step, 8)
        scale = pltpu.reciprocal(pivot, approx=True)
        if step + 1 < STEP:
            next_piece, next_index = divmod(step + 1, 8)
            cross = spread_row(pivots[step][next_piece], next_index) * spread_row(
                pivots[step + 1][piece], index
            )
            pivot = spread_row(pivots[step + 1][next_piece], next_index) - cross * scale
        own = sub == index
        factors = [
            (jnp.where(own, -1.0, pivots[step][at]) if at == piece else pivots[step][at]) * scale
            for at in pieces
        ]

        def reduce(column):
            row = spread_row(column[piece], index)
            return [
                (jnp.where(own, 0.0, column[at]) if at == piece else column[at]) - factors[at] * row
                for at in pieces
            ]

        panel = reduce(panel)
        for later in range(step + 1, STEP):
            pivots[later] = reduce(pivots[later])
    return panel


def sweep(matrix, first, last, tick=lambda: None):
    size = matrix.shape[0]
    pieces = range(STEP // 8)
    lane = lax.broadcasted_iota(jnp.int32, (8, size), 1)
    sub = lax.broadcasted_iota(jnp.int32, (8, size), 0)
    lane_all = lax.broadcasted_iota(jnp.int32, (size, size), 1)
    sub_all = lax.broadcasted_iota(jnp.int32, (size, size), 0)
    rows = [matrix[first + 8 * at : first + 8 * at + 8] for at in pieces]
    for start in range(first, last, STEP):
        stop = start + STEP
        more = stop < size
        pivots = [
            [jnp.broadcast_to(rows[at][:, start + index : start + index + 1], (8, size)) for at in pieces]
            for index in range(STEP)
        ]
        inside = (lane >= start) & (lane < stop)
        panel = [
            jnp.where(inside, jnp.where(lane - start == sub + 8 * at, 1.0, 0.0), rows[at])
            for at in pieces
        ]
        row_inside = (sub_all >= start) & (sub_all < stop)
        lane_inside = (lane_all >= start) & (lane_all < stop)
        column = jnp.where(row_inside, 0.0, matrix)[:, start:stop]
        base = jnp.where(row_inside | lane_inside, 0.0, matrix)
        following = []
        if more:
            following = [matrix[stop + 8 * at : stop + 8 * at + 8] for at in pieces]
        ahead = [
            [jnp.broadcast_to(piece[:, start + index : start + index + 1], (8, size)) for piece in following]
            for index in range(STEP)
        ]
        tick()
        panel = eliminate(panel, pivots)
        if more:
            rows = []
            for at in pieces:
                terms = [
                    ahead[index][at] * spread_row(panel[index // 8], index % 8)
                    for index in range(STEP)
                ]
                while len(terms) > 1:
                    terms = [terms[at2] + terms[at2 + 1] for at2 in range(0, len(terms), 2)]
                rows.append(base[stop + 8 * at : stop + 8 * at + 8] - terms[0])
        joined = jnp.concatenate(panel, axis=0)
        matrix = base - jnp.dot(left6(column), right6(joined, 0), preferred_element_type=F32)
        parts = [matrix[:start]] if start else []
        parts.append(joined)
        if more:
            parts += rows
        if stop + (STEP if more else 0) < size:
            parts.append(matrix[stop + STEP :])
        matrix = jnp.concatenate(parts, axis=0)
    return matrix


def inverse(matrix, tick=lambda: None):
    return sweep(matrix, 0, matrix.shape[0], tick)


def add_eye(matrix):
    row = lax.broadcasted_iota(jnp.int32, matrix.shape, 0)
    column = lax.broadcasted_iota(jnp.int32, matrix.shape, 1)
    return matrix + jnp.where(row == column, 1.0, 0.0)


def gram_pair(levels, width, count, level, v6_ref, s6_ref):
    low = level * width
    pair = min(2, levels - level)
    product = dot6_nt(v6_ref[low:, :], s6_ref[low : low + pair * width, :])
    result = []
    for index in range(pair):
        value = product[index * width : count - low, index * width : (index + 1) * width]
        offset = sum(count - done * width for done in range(level + index)) - width
        if offset < 0:
            result.append((offset, value[:width]))
            value = value[width:]
            offset = 0
        result.append((offset, value))
    return result


def leaf_kernel(levels, width, blocks, place_ref, ranks_hbm, rhs_hbm, leaf_hbm, bases_hbm, *refs):
    key_ref, rest_ref, scaled_ref, lower_ref, v6_ref, s6_ref, v_ref, *refs = refs
    ranks_ref, rhs_ref, leaf_ref, bases_ref, sem = refs
    nrhs = rhs_ref.shape[0]
    place = place_ref[0]
    rows = levels * width
    count = rows + nrhs
    padded = v6_ref.shape[0]
    spans = [slice(block * width, (block + 1) * width) for block in range(blocks)]
    leaf_copies = [
        pltpu.make_async_copy(leaf_hbm.at[span], leaf_ref.at[span], sem.at[index])
        for index, span in enumerate(spans)
    ]
    other_copies = [
        pltpu.make_async_copy(bases_hbm, bases_ref, sem.at[blocks]),
        pltpu.make_async_copy(rhs_hbm, rhs_ref, sem.at[blocks + 1]),
        pltpu.make_async_copy(ranks_hbm, ranks_ref, sem.at[blocks + 2]),
    ]
    for copy in leaf_copies + other_copies:
        copy.start()

    tasks = []
    quota = [0]

    def tick():
        for _ in range(min(quota[0], len(tasks))):
            tasks.pop(0)()

    def run(steps):
        quota[0] = -(-len(tasks) // steps)

    def arrive():
        for copy in leaf_copies[1:] + other_copies:
            copy.wait()

    def load(block, level):
        sub = lax.broadcasted_iota(jnp.int32, (width, width), 0)
        rank = ranks_ref[2 ** (levels - level) + lax.shift_right_logical(place, level) - 1]
        piece = jnp.where(sub < rank, bases_ref[level - 1, spans[block], :].T, 0.0)
        span = slice((level - 1) * width, level * width)
        v_ref[block, span, :] = piece
        if block == 0:
            v6_ref[span, :] = left6(piece)

    def load_rhs():
        for block, span in enumerate(spans):
            piece = rhs_ref[:, span]
            piece = jnp.concatenate([piece, jnp.zeros((padded - count, width), F32)], axis=0)
            v_ref[block, rows:padded, :] = piece
            if block == 0:
                v6_ref[rows:padded, :] = left6(piece)

    chunk = up(padded // 3, 16)
    chunks = [slice(at, min(at + chunk, padded)) for at in range(0, padded, chunk)]

    def split_values(block, span):
        v6_ref[span, :] = left6(v_ref[block, span, :])

    def apply(block, weights, span):
        product = jnp.dot(v6_ref[span, :], weights, preferred_element_type=F32)
        scaled = product[:, :width]
        scaled_ref[block, span, :] = scaled
        stop = min(span.stop, rows)
        if span.start < stop:
            s6_ref[span.start : stop, :] = right6(scaled[: stop - span.start], 1)
        for later in range(block + 1, blocks):
            at = (later - block) * width
            v_ref[later, span, :] = v_ref[later, span, :] - product[:, at : at + width]

    def gram(block, level):
        for offset, value in gram_pair(levels, width, count, level, v6_ref, s6_ref):
            target = key_ref if offset < 0 else rest_ref
            span = slice(max(offset, 0), max(offset, 0) + value.shape[0])
            target[span, :] = value if block == 0 else target[span, :] + value

    leaf_copies[0].wait()
    tasks.append(arrive)
    tasks += [functools.partial(load, 0, level) for level in range(1, levels + 1)]
    tasks.append(load_rhs)
    for block in range(1, blocks):
        tasks += [functools.partial(load, block, level) for level in range(1, levels + 1)]
    schur = {(0, 0): leaf_ref[spans[0], spans[0]]}
    for block in range(blocks):
        run(width // STEP)
        inv = inverse(schur[block, block], tick)
        while tasks:
            tasks.pop(0)()
        if block == 0:
            for first in range(blocks):
                for second in range(blocks):
                    if first or second:
                        schur[first, second] = leaf_ref[spans[first], spans[second]]
        rest = range(block + 1, blocks)
        weights = right6(inv, 0)
        if rest:
            right = jnp.concatenate([schur[block, later] for later in rest], axis=1)
            upper = dot(inv, right)
            split = right6(upper, 0)
            for index, later in enumerate(rest):
                lower_ref[block, later - 1] = upper[:, index * width : (index + 1) * width]

            def reduce(first, block=block, rest=rest, split=split):
                product = jnp.dot(left6(schur[first, block]), split, preferred_element_type=F32)
                for index, later in enumerate(rest):
                    at = slice(index * width, (index + 1) * width)
                    schur[first, later] = schur[first, later] - product[:, at]

            reduce(block + 1)
            tasks += [functools.partial(reduce, first) for first in rest[1:]]
            weights = jnp.concatenate([weights, split], axis=1)
        if block:
            tasks += [functools.partial(split_values, block, span) for span in chunks]
        tasks += [functools.partial(apply, block, weights, span) for span in chunks]
        if block < blocks - 1:
            tasks += [functools.partial(gram, block, level) for level in range(0, levels, 2)]
    while tasks:
        tasks.pop(0)()
    key = dot6_nt(v6_ref[:width, :], s6_ref[:width, :])
    key_ref[...] = key_ref[...] + key if blocks > 1 else key
    if blocks == 1:
        rest_ref[...] = jnp.zeros_like(rest_ref)


def gram_kernel(levels, width, count, part_ref, v6_ref, s6_ref, rest_ref):
    for level in range(0, levels, 2):
        for offset, value in gram_pair(levels, width, count, level, v6_ref, s6_ref):
            if offset >= 0:
                span = slice(offset, offset + value.shape[0])
                rest_ref[span, :] = part_ref[span, :] + value


def pivot_kernel(first, last, *refs):
    if first == 0:
        matrix = add_eye(refs[0][...] + refs[1][...])
    else:
        matrix = refs[0][...]
    refs[-1][...] = sweep(matrix, first, last)


def near_update(width, count, take, *refs):
    rest_ref, coef_ref, key_ref = refs[-3:]
    inv_ref = refs[-4]
    take(refs[:-4], rest_ref)
    coef_ref[...] = dot(rest_ref[:count], inv_ref[...])
    next_key(width, count, rest_ref, coef_ref, key_ref)


def last_update(width, count, own_ref, other_ref, inv_ref, coef_ref, last_ref):
    rest = own_ref[:count] + other_ref[:count]
    coef_ref[...] = dot(rest, inv_ref[...])
    total = own_ref[count:] + other_ref[count:]
    last_ref[...] = total - dot_nt(coef_ref[...], rest[:width])


def next_key(width, count, rest_ref, coef_ref, key_ref):
    key_ref[...] = rest_ref[count : count + width] - dot_nt(coef_ref[:width], rest_ref[:width])


def take_full(refs, rest_ref):
    own_ref, other_ref = refs
    rows = rest_ref.shape[0]
    rest_ref[...] = own_ref[:rows] + other_ref[:rows]


def take_halves(plan, refs, rest_ref):
    place_ref, own_ref, near_ref, cross_ref = refs
    side = place_ref[0] & 1
    for index, source in ((side, near_ref), (side ^ 1, cross_ref)):
        span = pl.ds(plan.near2_at(index), plan.near2)
        rest_ref[span, :] = own_ref[span, :] + source[...]


def take_quarters(plan, refs, rest_ref):
    place_ref, joined_ref, cross_ref = refs
    for index in range(4):
        source, at = (joined_ref, cross_ref)[index & 1], (index // 2) * plan.near3
        span = pl.ds(plan.near3_at((place_ref[0] & 3) ^ index), plan.near3)
        rest_ref[span, :] = source[at : at + plan.near3, :]


def rank_update(width, count, below, first, last, rest_ref, coef_ref, put):
    offset = 0
    for level in range(below):
        low = level * width
        start = low + width if level == 0 else low
        size = count - start
        begin, end = max(first - offset, 0), min(last - offset, size)
        if begin < end:
            product = dot_nt(coef_ref[start + begin : start + end, :], rest_ref[low : low + width, :])
            put(offset + begin, product)
        offset += size


def far_update(width, count, below, own_ref, other_ref, rest_ref, coef_ref, out_ref):
    skip = count + width

    def put(offset, product):
        span = slice(skip + offset, skip + offset + product.shape[0])
        out_ref[offset : offset + product.shape[0], :] = own_ref[span, :] + other_ref[span, :] - product

    rank_update(width, count, below, 0, out_ref.shape[0], rest_ref, coef_ref, put)


def part_update(plan, width, count, below, first, place_ref, *refs):
    own_ref, other_ref, rest_ref, coef_ref, out_ref, *send_refs = refs
    skip = count + width
    place = place_ref[0]

    def put(offset, product):
        span = slice(skip + offset, skip + offset + product.shape[0])
        at = offset - first
        out_ref[at : at + product.shape[0], :] = own_ref[span, :] + other_ref[span, :] - product

    rank_update(width, count, below, first, first + out_ref.shape[0], rest_ref, coef_ref, put)
    if first == 0:
        send_refs[0][...] = out_ref[pl.ds(plan.near2_at(place & 1), plan.near2), :]
    else:
        send_refs[0][...] = out_ref[pl.ds(plan.near3_at((place & 3) ^ 2), plan.near3), :]
        send_refs[1][...] = out_ref[pl.ds(plan.rows3 + plan.far3_at(place & 1), plan.far3), :]


def quarter_update(plan, width, count, below, *refs):
    place_ref, own_ref, near_ref, cross_ref, far_own_ref, far_ref, inv_ref = refs[:7]
    rest_ref, coef_ref, out_ref, product_ref = refs[7:]
    take_halves(plan, (place_ref, own_ref, near_ref, cross_ref), rest_ref)
    coef_ref[...] = dot(rest_ref[:count], inv_ref[...])

    def put(offset, product):
        product_ref[offset : offset + product.shape[0], :] = product

    rank_update(width, count, below, 0, plan.rows3, rest_ref, coef_ref, put)
    span = pl.ds(plan.near3_at(place_ref[0] & 3), plan.near3)
    out_ref[...] = far_own_ref[span, :] + far_ref[...] - product_ref[span, :]


def half_update(plan, width, count, below, *refs):
    place_ref, rest_ref, coef_ref, own_ref, far_ref, out_ref, product_ref = refs

    def put(offset, product):
        at = offset - plan.rows3
        product_ref[at : at + product.shape[0], :] = product

    rank_update(width, count, below, plan.rows3, plan.far, rest_ref, coef_ref, put)
    at = plan.far3_at(place_ref[0] & 1)
    out_ref[...] = (
        own_ref[pl.ds(plan.rows3 + at, plan.far3), :]
        + far_ref[...]
        - product_ref[pl.ds(at, plan.far3), :]
    )


def joined_update(plan, width, count, below, *refs):
    place_ref, half_ref, cross_ref, rest_ref, coef_ref, out_ref, total_ref = refs
    side = place_ref[0] & 1
    for index, source in ((side, half_ref), (side ^ 1, cross_ref)):
        total_ref[pl.ds(plan.far3_at(index), plan.far3), :] = source[2 * plan.near3 :, :]

    def put(offset, product):
        span = slice(offset, offset + product.shape[0])
        out_ref[span, :] = total_ref[span, :] - product

    rank_update(width, count, below, 0, out_ref.shape[0], rest_ref, coef_ref, put)


def add_kernel(own_ref, other_ref, out_ref):
    out_ref[...] = own_ref[...] + other_ref[...]


def join_kernel(first_ref, second_ref, own_ref, other_ref, out_ref):
    rows = first_ref.shape[0]
    out_ref[:rows] = first_ref[...]
    out_ref[rows : 2 * rows] = second_ref[...]
    out_ref[2 * rows :] = own_ref[...] + other_ref[...]


def back_kernel(width, blocks, scaled_ref, lower_ref, out_ref):
    values = [None] * blocks
    for block in reversed(range(blocks)):
        value = scaled_ref[block]
        for later in range(block + 1, blocks):
            value = value - dot_nt(values[later], lower_ref[block, later - 1])
        values[block] = value
        out_ref[:, block * width : (block + 1) * width] = value


def fold_kernel(levels, width, nrhs, weights_ref, *refs):
    coef_refs, out_ref = refs[:-1], refs[-1]
    known = [None] * (levels - 1)
    for level in reversed(range(levels - 1)):
        coef = coef_refs[level]
        value = coef[(levels - 2 - level) * width :, :]
        above = range(level + 1, levels - 1)
        if above:
            value = value - dot(
                jnp.concatenate([known[later] for later in above], axis=1),
                coef[: len(above) * width, :],
            )
        known[level] = value
    low = (levels - 1) * width
    out_ref[...] = weights_ref[low : low + width + nrhs, :] - dot(
        jnp.concatenate(known, axis=1), weights_ref[:low, :]
    )


def final_kernel(width, own_ref, other_ref, folded_ref, out_ref):
    inv = inverse(add_eye(own_ref[:width] + other_ref[:width]))
    coef = dot(own_ref[width:] + other_ref[width:], inv)
    out_ref[...] = folded_ref[width:, :] - dot(coef, folded_ref[:width, :])


def call(kernel, shapes, *operands, cost=1.5, smem=0, hbm=0, scratch=(), limit=VMEM_LIMIT):
    flops = int(cost * 10**9)
    space = [pl.BlockSpec(memory_space=pltpu.SMEM)] * smem
    space += [pl.BlockSpec(memory_space=pltpu.VMEM)] * (len(operands) - smem - hbm)
    space += [pl.BlockSpec(memory_space=pltpu.HBM)] * hbm
    outs = [
        shape if isinstance(shape, jax.ShapeDtypeStruct) else jax.ShapeDtypeStruct(shape, F32)
        for shape in shapes
    ]
    return pl.pallas_call(
        kernel,
        out_shape=outs,
        in_specs=space,
        out_specs=[pl.BlockSpec(memory_space=pltpu.VMEM)] * len(outs),
        scratch_shapes=list(scratch),
        compiler_params=pltpu.CompilerParams(vmem_limit_bytes=limit),
        cost_estimate=pl.CostEstimate(flops=flops, bytes_accessed=flops // 300, transcendentals=0),
    )(*operands)


def flip(value, mask, axis="rowb"):
    pairs = [(source, source ^ mask) for source in range(lax.axis_size(axis))]
    return lax.ppermute(value, axis, pairs)


def partner(value, level, inner_bits):
    if level < inner_bits:
        return flip(value, 2**level)
    return flip(value, 2 ** (level - inner_bits), "rowa")


def up(value, step):
    return -(-value // step) * step


class Plan:
    def __init__(self, near, rows3, last3):
        self.near, self.rows3, self.last3, self.far = near, rows3, last3, rows3 + last3
        self.near2 = up(near, 16) // 2
        self.near3 = up(rows3, 32) // 4
        self.far3 = up(last3, 16) // 2

    def near2_at(self, side):
        return pl.multiple_of(side * (self.near - self.near2), 8)

    def near3_at(self, index):
        return pl.multiple_of(jnp.minimum(index * self.near3, self.rows3 - self.near3), 8)

    def far3_at(self, side):
        return pl.multiple_of(side * (self.last3 - self.far3), 8)


def body(right_side, leaves, bases, ranks):
    levels = bases.shape[0]
    leaf_rows = leaves.shape[0]
    width = bases.shape[2]
    nrhs = right_side.shape[1]
    blocks = leaf_rows // width
    inner_bits = lax.axis_size("rowb").bit_length() - 1
    place = lax.axis_index("rowa") * lax.axis_size("rowb") + lax.axis_index("rowb")
    place = place.astype(jnp.int32).reshape(1)
    rows = levels * width + nrhs
    padded = up(rows, 16)
    counts = [rows - level * width for level in range(levels)]
    spread = inner_bits >= 3 and levels >= 4
    plan = None
    if spread:
        plan = Plan(counts[1], counts[2], sum(counts[3:]) - width)
    square = (width, width)
    middle = up(width // 2, STEP)
    key, part, scaled, lower, values6, scaled6 = call(
        functools.partial(leaf_kernel, levels, width, blocks),
        [
            square,
            (sum(counts) - width, width),
            (blocks, padded, width),
            (blocks, max(blocks - 1, 1)) + square,
            jax.ShapeDtypeStruct((padded, 6 * width), BF16),
            jax.ShapeDtypeStruct((levels * width, 6 * width), BF16),
        ],
        place,
        *[
            pltpu.with_memory_space_constraint(each, pltpu.HBM)
            for each in (ranks, right_side.T, leaves, bases)
        ],
        smem=1,
        hbm=4,
        limit=LEAF_LIMIT,
        scratch=[
            pltpu.VMEM((blocks, padded, width), F32),
            pltpu.SMEM(ranks.shape, jnp.int32),
            pltpu.VMEM((nrhs, leaf_rows), F32),
            pltpu.VMEM((leaf_rows, leaf_rows), F32),
            pltpu.VMEM((levels, leaf_rows, width), F32),
            pltpu.SemaphoreType.DMA((blocks + 3,)),
        ],
    )
    (rest,) = call(
        functools.partial(gram_kernel, levels, width, rows),
        [(sum(counts) - width, width)],
        part,
        values6,
        scaled6,
    )
    if not spread:
        (weights,) = call(
            functools.partial(back_kernel, width, blocks), [(padded, leaf_rows)], scaled, lower
        )
    coefs = []
    for level in range(levels - 1):
        count = counts[level] - width
        below = levels - 1 - level
        following = sum(counts[level + 1 :]) - width
        if spread and level == 1:
            other_key = partner(key, level, inner_bits)
            near = partner(mine, level, inner_bits)
            far = partner(send, level, inner_bits)
            (half,) = call(functools.partial(pivot_kernel, 0, middle), [square], key, other_key)
            send_last, half = lax.optimization_barrier((send_last, half))
            far_last = partner(send_last, level, inner_bits)
            half, near = lax.optimization_barrier((half, near))
            cross = flip(near, 1)
            (inv,) = call(functools.partial(pivot_kernel, middle, width), [square], half)
            total, coef, quarter = call(
                functools.partial(quarter_update, plan, width, count, below),
                [(plan.near, width), (count, width), (plan.near3, width)],
                place,
                rest_near,
                near,
                cross,
                rest_far,
                far,
                inv,
                smem=1,
                scratch=[pltpu.VMEM((plan.rows3, width), F32)],
            )
            (key,) = call(functools.partial(next_key, width, count), [square], total, coef, cost=0.3)
        elif spread and level == 2:
            other_quarter = partner(quarter, level, inner_bits)
            other_key = partner(key, level, inner_bits)
            (last_half,) = call(
                functools.partial(half_update, plan, width, counts[1] - width, levels - 2),
                [(plan.far3, width)],
                place,
                total,
                coefs[1],
                rest_far,
                far_last,
                cost=0.3,
                smem=1,
                scratch=[pltpu.VMEM((plan.last3, width), F32)],
            )
            other_half = partner(last_half, level, inner_bits)
            other_quarter, _ = lax.optimization_barrier((other_quarter, last_half))
            (quarter,) = call(add_kernel, [quarter.shape], quarter, other_quarter, cost=0.1)
            opposite = flip(quarter, 2)
            scaled, _ = lax.optimization_barrier((scaled, quarter))
            (weights,) = call(
                functools.partial(back_kernel, width, blocks),
                [(padded, leaf_rows)],
                scaled,
                lower,
                cost=1.0,
            )
            other_key, weights = lax.optimization_barrier((other_key, weights))
            (half,) = call(functools.partial(pivot_kernel, 0, middle), [square], key, other_key)
            half, opposite, other_half = lax.optimization_barrier((half, opposite, other_half))
            (joined,) = call(
                join_kernel,
                [(2 * plan.near3 + plan.far3, width)],
                quarter,
                opposite,
                last_half,
                other_half,
                cost=0.1,
            )
            joined_cross = flip(joined, 1)
            (inv,) = call(functools.partial(pivot_kernel, middle, width), [square], half)
            total, coef, key = call(
                functools.partial(
                    near_update, width, count, functools.partial(take_quarters, plan)
                ),
                [(plan.rows3, width), (count, width), square],
                place,
                joined,
                joined_cross,
                inv,
                smem=1,
            )
            (rest,) = call(
                functools.partial(joined_update, plan, width, count, below),
                [(following, width)],
                place,
                joined,
                joined_cross,
                total,
                coef,
                smem=1,
                scratch=[pltpu.VMEM((plan.last3, width), F32)],
            )
        else:
            other_key = partner(key, level, inner_bits)
            sent_rest = rest
            if level == 0:
                sent_rest, other_key = lax.optimization_barrier((rest, other_key))
            other_rest = partner(sent_rest, level, inner_bits)
            (inv,) = call(functools.partial(pivot_kernel, 0, width), [square], key, other_key)
            if level == levels - 2:
                coef, last = call(
                    functools.partial(last_update, width, count),
                    [(count, width), (counts[level + 1], width)],
                    rest,
                    other_rest,
                    inv,
                )
                coefs.append(coef)
                continue
            total, coef, key = call(
                functools.partial(near_update, width, count, take_full),
                [(counts[level], width), (count, width), square],
                rest,
                other_rest,
                inv,
            )
            if spread and level == 0:
                parts = []
                for first, size, sent in (
                    (0, plan.near, [plan.near2]),
                    (plan.near, plan.far, [plan.near3, plan.far3]),
                ):
                    parts += call(
                        functools.partial(part_update, plan, width, count, below, first),
                        [(each, width) for each in [size] + sent],
                        place,
                        rest,
                        other_rest,
                        total,
                        coef,
                        cost=0.4,
                        smem=1,
                    )
                    total, _ = lax.optimization_barrier((total, parts[-1]))
                rest_near, mine, rest_far, send, send_last = parts
            else:
                (rest,) = call(
                    functools.partial(far_update, width, count, below),
                    [(following, width)],
                    rest,
                    other_rest,
                    total,
                    coef,
                )
        coefs.append(coef)
    other_last = partner(last, levels - 1, inner_bits)
    (folded,) = call(
        functools.partial(fold_kernel, levels, width, nrhs),
        [(width + nrhs, leaf_rows)],
        weights,
        *coefs,
    )
    (result,) = call(
        functools.partial(final_kernel, width), [(nrhs, leaf_rows)], last, other_last, folded
    )
    return result.T


def solution(mesh):
    placed = (
        P(("rowa", "rowb"), None),
        P(("rowa", "rowb"), None),
        P(None, ("rowa", "rowb"), None),
        P(),
    )
    return jax.shard_map(
        body, mesh=mesh, in_specs=placed, out_specs=P(("rowa", "rowb"), None), check_vma=False
    )
```
